128 devices in a mesh: row: 8 (over z_lo, x), col: 16 (over y, z_hi, core).
Axes of the slice: x: 4, y: 4, z: 4 (z_hi: 2, z_lo: 2; z = z_hi * 2 + z_lo), core: 2. Of those that a mesh axis runs over, the one named last changes fastest.
Arguments:
- inputs: bfloat16 [1024, 12288], P('row', 'col'), may hold values from -6 to 6
- pre_act: bfloat16 [1024, 24576], P('col', 'row'), may hold values from -6 to 6
- w_first: bfloat16 [12288, 24576], P('col', 'row'), may hold values from -0.0546875 to 0.0546875
- w_second: bfloat16 [24576, 12288], P('row', 'col'), may hold values from -0.0390625 to 0.0390625
- out_grad: bfloat16 [1024, 12288], P('row', 'col'), may hold values from -1.0546875 to 1.0546875
Outputs:
- input_grad: bfloat16 [1024, 12288], P('row', 'col')
- first_grad: bfloat16 [12288, 24576], P('col', 'row')
- second_grad: bfloat16 [24576, 12288], P('row', 'col')
The draws below stay inside these ranges and needn't reach their ends.
All inputs are finite; a program needn't handle non-finite values.
Results may differ from the reference program's by a relative error of at most 0.025.
Values may be sent and summed in bfloat16 or wider, within the bound.
A program may use at most 128 MiB of HBM per device.

```python
import jax
import jax.numpy as jnp
from jax import lax

D = 12288
FF = 24576
TOKENS = 1024
N_COL = 16


def shard_levels(key, dims, split, smallest, largest):
    level, own = 1.0, jax.random.fold_in(key, 6)
    for position, shards_of in split:
        draws = jnp.exp(jax.random.uniform(jax.random.fold_in(own, position), (shards_of,), jnp.float32, smallest / len(split), largest / len(split)))
        level = level * jnp.repeat(draws, dims[position] // shards_of).reshape([-1 if axis == position else 1 for axis in range(len(dims))])
    return level


def normal_values(key, shape, deviation, limit, shards=(), dtype=jnp.bfloat16):
    drawn = jax.random.normal(key, shape, jnp.float32) * deviation
    if len(shards) > 0:
        drawn = shard_levels(key, shape, shards, -0.22, 0.18) * drawn
    return jnp.clip(drawn, min=-limit, max=limit).astype(dtype)


def setup_inputs(seed: int = 0) -> dict:
    arg_keys = jax.random.split(jax.random.key(seed), 6)
    return {
        "inputs": normal_values(arg_keys[0], (TOKENS, D), 1.0, 6.0, ((0, 8), (1, 16))),
        "pre_act": normal_values(arg_keys[1], (TOKENS, FF), 1.0, 6.0, ((0, 16), (1, 8))),
        "w_first": normal_values(arg_keys[2], (D, FF), D ** -0.5, 0.0546875, ((0, 16), (1, 8))),
        "w_second": normal_values(arg_keys[3], (FF, D), FF ** -0.5, 0.0390625, ((0, 8), (1, 16))),
        "out_grad": normal_values(arg_keys[4], (TOKENS, D), (TOKENS ** -0.25), 1.0546875, ((0, 8), (1, 16))),
    }


def gelu_back(pre32, grad32):
    values, pullback = jax.vjp(lambda v: jax.nn.gelu(v, approximate=True), pre32)
    return (values, pullback(grad32)[0])

def reference(inputs, pre_act, w_first, w_second, out_grad):
    group = D // N_COL

    def add_group(k, total):
        start = (k * group).astype(jnp.int32)
        grad_part = lax.dynamic_slice_in_dim(out_grad, start, group, 1)
        weight_part = lax.dynamic_slice_in_dim(w_second, start, group, 1)
        term = lax.dot_general(grad_part, weight_part, (((1,), (1,)), ((), ())), preferred_element_type=jnp.float32)
        term = lax.optimization_barrier(term.astype(jnp.bfloat16))
        return total + term.astype(jnp.float32)
    summed = lax.fori_loop(jnp.int32(0), jnp.int32(N_COL), add_group, jnp.zeros((TOKENS, FF), jnp.float32))
    hidden_grad = summed.astype(jnp.bfloat16)
    values, slope = gelu_back(pre_act.astype(jnp.float32), hidden_grad.astype(jnp.float32))
    activated = values.astype(jnp.bfloat16)
    pre_grad = slope.astype(jnp.bfloat16)
    second_grad = lax.dot_general(activated, out_grad, (((0,), (0,)), ((), ())), preferred_element_type=jnp.float32)
    first_grad = lax.dot_general(inputs, pre_grad, (((0,), (0,)), ((), ())), preferred_element_type=jnp.float32)
    input_grad = lax.dot_general(pre_grad, w_first, (((1,), (1,)), ((), ())), preferred_element_type=jnp.float32)
    return (input_grad.astype(jnp.bfloat16), first_grad.astype(jnp.bfloat16), second_grad.astype(jnp.bfloat16))
```

```python
import jax
import jax.numpy as jnp
from jax import lax
from jax.experimental import pallas as pl
from jax.experimental.pallas import tpu as pltpu
from jax.sharding import PartitionSpec as P

MESH = pl.DeviceIdType.MESH
T = 128
W = 768
BF = jnp.bfloat16
F32 = jnp.float32
ROOT = 0.7978845608028654
CUBE = 0.044715


def rows(block):
    return pl.ds(pl.multiple_of(block * T, T), T)


def rt_dot(left, right):
    return lax.dot_general(left, right, (((1,), (1,)), ((), ())), preferred_element_type=F32)


def tl_dot(left, right):
    return lax.dot_general(left, right, (((0,), (0,)), ((), ())), preferred_element_type=F32)


class Group:
    def __init__(self, g, h, device, block):
        self.g, self.h = g, h
        self.above, self.below, self.pair = device((g + 1) % 4, h), device((g + 3) % 4, h), device(g, 1 - h)
        self.block = lambda dg, other: block((g + dg) % 4, (1 - h) if other else h)


class Gather:
    OWNER = ((0, True), (3, False), (1, False), (3, True), (1, True), (2, False), (2, True))

    def __init__(self, group, buf, mate_buf, mate, ssem, rsem, own_src=None):
        self.group, self.buf, self.mate_buf, self.mate = group, buf, mate_buf, mate
        self.ssem, self.rsem, self.own_src = ssem, rsem, own_src
        self.sent = []

    def _copy(self, slot, owner, device, src=None):
        at = rows(self.group.block(*owner))
        return pltpu.make_async_remote_copy(
            self.buf.at[at] if src is None else src, self.buf.at[at],
            self.ssem.at[slot], self.rsem.at[slot], device, MESH)

    def _send(self, slot, owner, device, src=None):
        c = self._copy(slot, owner, device, src)
        c.start()
        self.sent.append(c)

    def _mate(self, index, owner, src=None):
        if self.mate is None:
            return
        at = rows(self.group.block(*owner))
        c = pltpu.make_async_remote_copy(
            self.buf.at[at] if src is None else src, self.buf.at[at],
            self.ssem.at[7 + index], self.rsem.at[7 + index], self.mate, MESH)
        c.start()
        self.sent.append(c)

    def start(self):
        g, own = self.group, (0, False)
        self._send(0, own, g.pair, self.own_src)
        self._send(1, own, g.above, self.own_src)
        self._send(2, own, g.below, self.own_src)
        self._mate(7, own, self.own_src)

    def take(self, slot):
        g, owner = self.group, self.OWNER[slot]
        self._copy(slot, owner, g.pair).wait_recv()
        if slot == 0:
            self._send(3, owner, g.above)
            self._send(4, owner, g.below)
        elif slot == 1:
            self._send(5, owner, g.above)
        elif slot == 4:
            self._send(6, owner, g.below)
        self._mate(slot, owner)

    def take_mate(self):
        for index, owner in enumerate(self.OWNER + ((0, False),)):
            at = rows(self.group.block(*owner))
            pltpu.make_async_remote_copy(
                self.mate_buf.at[at], self.mate_buf.at[at],
                self.ssem.at[7 + index], self.rsem.at[7 + index], self.mate, MESH).wait_recv()

    def drain(self):
        for c in self.sent:
            c.wait_send()


class Scatter:
    def __init__(self, group, part, rbuf, ssem, rsem):
        self.group, self.part, self.rbuf, self.ssem, self.rsem = group, part, rbuf, ssem, rsem
        self.sent = []

    def at(self, dg, other):
        return rows(self.group.block(dg, other))

    def _copy(self, slot, at, device):
        return pltpu.make_async_remote_copy(
            self.part.at[at], self.rbuf.at[slot], self.ssem.at[slot], self.rsem.at[slot], device, MESH)

    def _send(self, slot, dg, other, device):
        c = self._copy(slot, self.at(dg, other), device)
        c.start()
        self.sent.append(c)

    def _wait(self, slot):
        self._copy(slot, self.at(0, False), self.group.pair).wait_recv()

    def far(self):
        self._send(0, 2, False, self.group.above)
        self._send(1, 2, True, self.group.below)

    def near(self):
        self._send(2, 1, True, self.group.above)
        self._send(3, 3, False, self.group.below)

    def fold(self):
        for slot, dg, other, device in ((0, 1, False, self.group.above), (1, 3, True, self.group.below)):
            self._wait(slot)
            at = self.at(dg, other)
            self.part[at] = (self.part[at].astype(F32) + self.rbuf[slot].astype(F32)).astype(BF)
            self._send(slot + 4, dg, other, device)

    def _total(self, other):
        direct, folded = (2, 5) if other else (3, 4)
        return (self.part[self.at(0, other)].astype(F32) + self.rbuf[direct].astype(F32)
                + self.rbuf[folded].astype(F32))

    def cross(self):
        self._wait(2)
        self._wait(5)
        self.part[self.at(0, True)] = self._total(True).astype(BF)
        self._send(6, 0, True, self.group.pair)

    def result(self):
        self._wait(3)
        self._wait(4)
        own = self._total(False)
        self._wait(6)
        return own + self.rbuf[6].astype(F32)

    def drain(self):
        for c in self.sent:
            c.wait_send()


def kernel(in_ref, pre_ref, w1_ref, w2_ref, og_ref, dx_ref, dw1_ref, dw2_ref,
           og_all, in_all, act_all, pre_all, pre_loc, slope, w1, w2, part, inp, acc, rbuf, out1, out2, dxv,
           g_ss, g_rs, r_ss, r_rs, k_ss, k_rs, l_sem, o_sem):
    r, c = lax.axis_index("row"), lax.axis_index("col")
    x, zl = r % 4, r // 4
    y, zh, k = c // 4, (c // 2) % 2, c % 2
    half = W * 2
    mate = (r, c + 1 - 2 * k)
    by_row = Group(x, zl, lambda g, h: (h * 4 + g, c), lambda g, h: h * 4 + g)
    by_col = Group(y, zh, lambda g, h: (r, g * 4 + h * 2 + k), lambda g, h: g * 2 + h)

    def cols(core, s):
        return pl.ds(pl.multiple_of(core * half + s * W, W), W)

    own64 = pl.ds(pl.multiple_of(k * 64, 64), 64)
    w2_rows = pl.ds(pl.multiple_of(k * half, half), half)
    w2_mate_rows = pl.ds(pl.multiple_of((1 - k) * half, half), half)
    loads = [
        pltpu.make_async_copy(pre_ref.at[:, cols(k, 0)], pre_loc.at[0, own64], l_sem.at[0]),
        pltpu.make_async_copy(pre_ref.at[:, cols(k, 1)], pre_loc.at[1, own64], l_sem.at[1]),
        pltpu.make_async_copy(og_ref, og_all.at[k, rows(r)], l_sem.at[2]),
        pltpu.make_async_copy(w2_ref.at[w2_rows], w2.at[k], l_sem.at[3]),
        pltpu.make_async_copy(in_ref, in_all.at[rows(r)], l_sem.at[4]),
        pltpu.make_async_copy(w1_ref, w1, l_sem.at[5]),
    ]
    for load in loads:
        load.start()

    barrier = pltpu.get_barrier_semaphore()
    friends = (mate, by_row.above, by_row.below, by_row.pair, by_col.above, by_col.below, by_col.pair)
    for friend in friends:
        pl.semaphore_signal(barrier, inc=1, device_id=friend, device_id_type=MESH)
    pl.semaphore_wait(barrier, len(friends))

    gathers = (
        Gather(by_row, og_all.at[k], og_all.at[1 - k], mate, g_ss.at[0], g_rs.at[0], og_ref),
        Gather(by_row, in_all, None, None, g_ss.at[1], g_rs.at[1], in_ref),
        Gather(by_col, act_all.at[2 * k], act_all.at[2 - 2 * k], mate, g_ss.at[2], g_rs.at[2]),
        Gather(by_col, act_all.at[2 * k + 1], act_all.at[3 - 2 * k], mate, g_ss.at[3], g_rs.at[3]),
        Gather(by_col, pre_all.at[2 * k], pre_all.at[2 - 2 * k], mate, g_ss.at[4], g_rs.at[4]),
        Gather(by_col, pre_all.at[2 * k + 1], pre_all.at[3 - 2 * k], mate, g_ss.at[5], g_rs.at[5]),
    )
    og, xs, act0, act1, pre0, pre1 = gathers
    hid = [Scatter(by_col, part.at[s], rbuf.at[s], r_ss.at[s], r_rs.at[s]) for s in range(2)]
    dx = Scatter(by_row, inp, rbuf.at[2], r_ss.at[2], r_rs.at[2])

    to_mate = [
        pltpu.make_async_remote_copy(pre_ref.at[:, cols(1 - k, 0)], pre_loc.at[0, own64], k_ss.at[0], k_rs.at[0], mate, MESH),
        pltpu.make_async_remote_copy(pre_ref.at[:, cols(1 - k, 1)], pre_loc.at[1, own64], k_ss.at[1], k_rs.at[1], mate, MESH),
        pltpu.make_async_remote_copy(w2_ref.at[w2_mate_rows], w2.at[k], k_ss.at[2], k_rs.at[2], mate, MESH),
    ]
    to_mate[0].start()
    to_mate[1].start()
    og.start()
    to_mate[2].start()

    def activate(s, gather):
        a = pre_loc[s].astype(F32)
        t = jnp.tanh(ROOT * (a + CUBE * (a * a * a)))
        act_all[2 * k + s, rows(by_col.block(0, False))] = (0.5 * a * (1.0 + t)).astype(BF)
        slope[s] = 0.5 * (1.0 + t) + 0.5 * a * (1.0 - t * t) * (ROOT * (1.0 + 3.0 * CUBE * (a * a)))

    def pre_grad(s):
        grad = hid[s].result().astype(BF).astype(F32)
        pre_all[2 * k + s, rows(by_col.block(0, False))] = (slope[s] * grad).astype(BF)

    def hidden(s, dg):
        at = pl.ds(pl.multiple_of(((y + dg) % 4) * 2 * T, 2 * T), 2 * T)

        def tile(n, _):
            units = pl.ds(pl.multiple_of(s * W + n * 256, 256), 256)
            to = pl.ds(pl.multiple_of(n * 256, 256), 256)
            part[s, at, to] = (rt_dot(og_all[0, at], w2[0, units]) + rt_dot(og_all[1, at], w2[1, units])).astype(BF)
            return 0

        lax.fori_loop(0, 3, tile, 0)

    def weight_grad(left, right, out, slot, dst):
        def tile(m, _):
            at = pl.ds(pl.multiple_of(m * 256, 256), 256)
            out[slot, at] = tl_dot(left[:, at], right[...]).astype(BF)
            return 0

        lax.fori_loop(0, 3, tile, 0)
        copy = pltpu.make_async_copy(out.at[slot], dst[0], dst[1])
        copy.start()
        return copy

    outs = []

    def second_grad(q):
        outs.append(weight_grad(act_all.at[q], og_all.at[k], out2, q, (dw2_ref.at[pl.ds(q * W, W)], o_sem.at[q])))

    def first_grad(q):
        outs.append(weight_grad(in_all, pre_all.at[q], out1, q, (dw1_ref.at[:, pl.ds(q * W, W)], o_sem.at[4 + q])))

    def input_early():
        def tile(m, _):
            at = pl.ds(pl.multiple_of(m * 256, 256), 256)
            acc[at] = (rt_dot(pre_all[0, at], w1[:, pl.ds(0, W)]) + rt_dot(pre_all[2, at], w1[:, pl.ds(2 * W, W)]))
            return 0

        lax.fori_loop(0, 4, tile, 0)

    def input_late(dg):
        for other in (False, True):
            at = rows(by_row.block(dg, other))

            def tile(n, _):
                to = pl.ds(pl.multiple_of(n * 256, 256), 256)
                inp[at, to] = (acc[at, to] + rt_dot(pre_all[1, at], w1[to, pl.ds(W, W)])
                               + rt_dot(pre_all[3, at], w1[to, pl.ds(3 * W, W)])).astype(BF)
                return 0

            lax.fori_loop(0, 3, tile, 0)

    loads[0].wait()
    to_mate[0].wait_recv()
    activate(0, act0)
    act0.start()
    loads[1].wait()
    to_mate[1].wait_recv()
    activate(1, act1)

    og.take(0)
    act0.take(0)
    for slot in (1, 2, 4, 3):
        og.take(slot)
        act0.take(slot)
    og.take(5)
    og.take(6)
    xs.start()
    loads[2].wait()
    loads[3].wait()
    to_mate[2].wait_recv()
    og.take_mate()

    hidden(0, 2)
    hid[0].far()
    hidden(0, 1)
    hidden(0, 3)
    hid[0].near()
    hidden(0, 0)
    act0.take(5)
    act0.take(6)
    hid[0].fold()
    hidden(1, 2)
    hid[1].far()
    hidden(1, 1)
    hidden(1, 3)
    hid[1].near()
    hidden(1, 0)
    xs.take(0)
    xs.take(1)
    xs.take(2)
    act0.take_mate()
    second_grad(0)
    hid[0].cross()
    hid[1].fold()
    xs.take(4)
    xs.take(3)
    second_grad(2)
    pre_grad(0)
    pre0.start()
    hid[1].cross()
    pre0.take(0)
    pre0.take(1)
    pre0.take(2)
    pre_grad(1)
    pre1.start()
    xs.take(5)
    xs.take(6)
    loads[4].wait()
    loads[5].wait()
    pre0.take(4)
    pre0.take(3)
    pre1.take(0)
    pre0.take(5)
    pre0.take(6)
    pre1.take(1)
    pre1.take(2)
    act1.start()
    pre0.take_mate()
    input_early()
    pre1.take(4)
    pre1.take(3)
    first_grad(0)
    act1.take(0)
    pre1.take(5)
    pre1.take(6)
    pre1.take_mate()

    input_late(2)
    dx.far()
    input_late(1)
    input_late(3)
    dx.near()
    input_late(0)
    act1.take(1)
    act1.take(2)
    first_grad(2)
    dx.fold()
    act1.take(4)
    act1.take(3)
    first_grad(1)
    dx.cross()
    act1.take(5)
    act1.take(6)
    first_grad(3)
    act1.take_mate()
    second_grad(1)
    second_grad(3)
    dxv[...] = dx.result().astype(BF)
    last = pltpu.make_async_copy(dxv, dx_ref, o_sem.at[8])
    last.start()
    for item in (*gathers, *hid, dx):
        item.drain()
    for copy in to_mate:
        copy.wait_send()
    for copy in outs:
        copy.wait()
    last.wait()


def local(inputs, pre_act, w_first, w_second, out_grad):
    sem = pltpu.SemaphoreType.DMA
    vm = lambda *shape, dtype=BF: pltpu.VMEM(shape, dtype)
    return pl.pallas_call(
        kernel,
        out_shape=(
            jax.ShapeDtypeStruct((T, W), BF),
            jax.ShapeDtypeStruct((W, 4 * W), BF),
            jax.ShapeDtypeStruct((4 * W, W), BF),
        ),
        in_specs=[pl.BlockSpec(memory_space=pl.ANY)] * 5,
        out_specs=[pl.BlockSpec(memory_space=pl.ANY)] * 3,
        scratch_shapes=[
            vm(2, 8 * T, W),
            vm(8 * T, W),
            vm(4, 8 * T, W),
            vm(4, 8 * T, W),
            vm(2, T, W),
            vm(2, T, W, dtype=F32),
            vm(W, 4 * W),
            vm(2, 2 * W, W),
            vm(2, 8 * T, W),
            vm(8 * T, W),
            vm(8 * T, W, dtype=F32),
            vm(3, 7, T, W),
            vm(4, W, W),
            vm(4, W, W),
            vm(T, W),
            sem((6, 15)), sem((6, 15)), sem((3, 7)), sem((3, 7)), sem((3,)), sem((3,)), sem((6,)), sem((9,)),
        ],
        compiler_params=pltpu.CompilerParams(
            collective_id=0, has_side_effects=True, vmem_limit_bytes=62 * 2**20
        ),
        cost_estimate=pl.CostEstimate(flops=19_327_352_832, bytes_accessed=20_000_000, transcendentals=400_000),
        name="ffn_back",
    )(inputs, pre_act, w_first, w_second, out_grad)


def solution(mesh):
    placed = (P("row", "col"), P("col", "row"), P("col", "row"), P("row", "col"), P("row", "col"))
    return jax.shard_map(
        local,
        mesh=mesh,
        in_specs=placed,
        out_specs=(P("row", "col"), P("col", "row"), P("row", "col")),
        check_vma=False,
    )
```

```python
import jax
import jax.numpy as jnp
from jax import lax
from jax.experimental import pallas as pl
from jax.experimental.pallas import tpu as pltpu
from jax.sharding import PartitionSpec as P

MESH = pl.DeviceIdType.MESH
T = 64
HALF = 512
W = 768
U = 1536
BF = jnp.bfloat16
F32 = jnp.float32
ROOT = 0.7978845608028654
CUBE = 0.044715


def dot(left, right):
    return jnp.dot(left, right, preferred_element_type=F32)


def tl_dot(left, right):
    return lax.dot_general(left, right, (((0,), (0,)), ((), ())), preferred_element_type=F32)


class Group:
    def __init__(self, g, h, device, block):
        self.g, self.h = g, h
        self.above, self.below, self.pair = device((g + 1) % 4, h), device((g + 3) % 4, h), device(g, 1 - h)
        self.block = lambda dg, other: block((g + dg) % 4, (1 - h) if other else h)


class Gather:
    def __init__(self, group, buf, mate_buf, mate, ssem, rsem, own_src=None):
        self.group, self.buf, self.mate_buf, self.mate = group, buf, mate_buf, mate
        self.ssem, self.rsem, self.own_src = ssem, rsem, own_src
        self.sent = []

    def _ref(self, buf, owner, part=None):
        at = pl.ds(pl.multiple_of(self.group.block(*owner) * T, T), T)
        if len(buf.shape) == 2:
            return buf.at[at]
        return buf.at[:, at] if part is None else buf.at[part, at]

    def _copy(self, slot, owner, device, part=None):
        ref = self._ref(self.buf, owner, part)
        own = owner == (0, False) and self.own_src is not None
        return pltpu.make_async_remote_copy(
            self.own_src if own else ref, ref, self.ssem.at[slot], self.rsem.at[slot], device, MESH)

    def _send(self, slot, owner, device, part=None):
        c = self._copy(slot, owner, device, part)
        c.start()
        self.sent.append(c)

    def _mate(self, owner):
        if self.mate is not None:
            self._send(8 + owner[0] * 2 + int(owner[1]), owner, self.mate)

    def take_mate(self):
        for dg in range(4):
            for other in (False, True):
                ref, slot = self._ref(self.mate_buf, (dg, other)), 8 + dg * 2 + int(other)
                pltpu.make_async_remote_copy(
                    ref, ref, self.ssem.at[slot], self.rsem.at[slot], self.mate, MESH).wait_recv()

    def drain(self):
        for c in self.sent:
            c.wait_send()


class PairFirst(Gather):
    OWNER = ((0, True), (3, False), (1, False), (3, True), (1, True), (2, False), (2, True))

    def start(self):
        g, own = self.group, (0, False)
        self._send(0, own, g.pair)
        self._send(1, own, g.above)
        self._send(2, own, g.below)
        self._mate(own)

    def take(self, *slots):
        g = self.group
        for slot in slots:
            owner = self.OWNER[slot]
            self._copy(slot, (owner[0], owner[1]), g.pair).wait_recv()
            if slot == 0:
                self._send(3, owner, g.above)
                self._send(4, owner, g.below)
            elif slot == 1:
                self._send(5, owner, g.above)
            elif slot == 4:
                self._send(6, owner, g.below)
            self._mate(owner)


class RingFirst(Gather):
    def start(self):
        g, own = self.group, (0, False)
        self._send(0, own, g.above)
        self._send(1, own, g.below)
        self._mate(own)

    def give_own(self):
        self._send(4, (0, False), self.group.pair)

    def take_near(self):
        g = self.group
        for slot, dg, on, part in ((0, 3, g.above, 0), (1, 1, g.below, 1)):
            owner = (dg, False)
            self._copy(slot, owner, g.pair).wait_recv()
            self._send(2 + part, owner, on, part)
            self._mate(owner)

    def give_near(self):
        self._send(5, (3, False), self.group.pair)
        self._send(6, (1, False), self.group.pair)

    def take_far(self):
        g, owner = self.group, (2, False)
        for part in (0, 1):
            self._copy(2 + part, owner, g.pair, part).wait_recv()
        self._mate(owner)

    def give_far(self):
        self._send(7, (2, False), self.group.pair)

    def take_pair(self, *places):
        for place in places:
            owner = ((0, 3, 1, 2)[place], True)
            self._copy(4 + place, owner, self.group.pair).wait_recv()
            self._mate(owner)


class Scatter:
    def __init__(self, group, part, rbuf, ssem, rsem):
        self.group, self.part, self.rbuf, self.ssem, self.rsem = group, part, rbuf, ssem, rsem
        self.sent = []

    def at(self, dg, other):
        return pl.ds(pl.multiple_of(self.group.block(dg, other) * T, T), T)

    def _copy(self, slot, at, device):
        return pltpu.make_async_remote_copy(
            self.part.at[at], self.rbuf.at[slot], self.ssem.at[slot], self.rsem.at[slot], device, MESH)

    def _send(self, slot, dg, other, device):
        c = self._copy(slot, self.at(dg, other), device)
        c.start()
        self.sent.append(c)

    def _wait(self, slot):
        self._copy(slot, self.at(0, False), self.group.pair).wait_recv()

    def far(self):
        self._send(0, 2, False, self.group.above)
        self._send(1, 2, True, self.group.below)

    def near(self):
        self._send(2, 1, True, self.group.above)
        self._send(3, 3, False, self.group.below)

    def fold(self):
        for slot, dg, other, device in ((0, 1, False, self.group.above), (1, 3, True, self.group.below)):
            self._wait(slot)
            at = self.at(dg, other)
            self.part[at] = (self.part[at].astype(F32) + self.rbuf[slot].astype(F32)).astype(BF)
            self._send(slot + 4, dg, other, device)

    def _total(self, other):
        direct, folded = (2, 5) if other else (3, 4)
        return (self.part[self.at(0, other)].astype(F32) + self.rbuf[direct].astype(F32)
                + self.rbuf[folded].astype(F32))

    def cross(self):
        self._wait(2)
        self._wait(5)
        self.part[self.at(0, True)] = self._total(True).astype(BF)
        self._send(6, 0, True, self.group.pair)

    def result(self):
        self._wait(3)
        self._wait(4)
        own = self._total(False)
        self._wait(6)
        return own + self.rbuf[6].astype(F32)

    def drain(self):
        for c in self.sent:
            c.wait_send()


def kernel(in_ref, pre_ref, w1_ref, w2_ref, og_ref, dxv, out1, out2,
           og_all, in_all, act_all, pre_all, pre_loc, slope, w1, w2, part, inp, rbuf, rbufx, w1t, w2t,
           g_ss, g_rs, r_ss, r_rs, k_ss, k_rs, l_sem):
    r, c = lax.axis_index("row"), lax.axis_index("col")
    x, zl = r % 4, r // 4
    y, zh, k = c // 4, (c // 2) % 2, c % 2
    mate = (r, c + 1 - 2 * k)
    by_row = Group(x, zl, lambda g, h: (h * 4 + g, c), lambda g, h: h * 4 + g)
    by_col = Group(y, zh, lambda g, h: (r, g * 4 + h * 2 + k), lambda g, h: g * 2 + h)
    mine_row = pl.ds(pl.multiple_of(r * T, T), T)
    mine_col = pl.ds(pl.multiple_of(by_col.block(0, False) * T, T), T)

    def units(core):
        return pl.ds(pl.multiple_of(core * U, U), U)

    loads = [
        pltpu.make_async_copy(pre_ref.at[:, units(k)], pre_loc.at[k], l_sem.at[0]),
        pltpu.make_async_copy(og_ref.at[pl.ds(0, T)], og_all.at[k, 0, mine_row], l_sem.at[1]),
        pltpu.make_async_copy(og_ref.at[pl.ds(T, T)], og_all.at[k, 1, mine_row], l_sem.at[2]),
        pltpu.make_async_copy(w2_ref.at[units(k)], w2.at[k], l_sem.at[3]),
        pltpu.make_async_copy(in_ref.at[pl.ds(0, T)], in_all.at[0, mine_row], l_sem.at[4]),
        pltpu.make_async_copy(in_ref.at[pl.ds(T, T)], in_all.at[1, mine_row], l_sem.at[5]),
        pltpu.make_async_copy(w1_ref, w1, l_sem.at[6]),
    ]
    for load in loads[:4]:
        load.start()

    barrier = pltpu.get_barrier_semaphore()
    friends = (mate, by_row.above, by_row.below, by_row.pair, by_col.above, by_col.below, by_col.pair)
    for friend in friends:
        pl.semaphore_signal(barrier, inc=1, device_id=friend, device_id_type=MESH)
    pl.semaphore_wait(barrier, len(friends))

    halves = (0, 1)
    og = [PairFirst(by_row, og_all.at[k, s], og_all.at[1 - k, s], mate, g_ss.at[s], g_rs.at[s],
                    og_ref.at[pl.ds(s * T, T)]) for s in halves]
    xs = [PairFirst(by_row, in_all.at[s], None, None, g_ss.at[2 + s], g_rs.at[2 + s],
                    in_ref.at[pl.ds(s * T, T)]) for s in halves]
    act = [RingFirst(by_col, act_all.at[k, f], act_all.at[1 - k, f], mate, g_ss.at[4 + f], g_rs.at[4 + f])
           for f in halves]
    pre = [PairFirst(by_col, pre_all.at[k, s], pre_all.at[1 - k, s], mate, g_ss.at[6 + s], g_rs.at[6 + s])
           for s in halves]
    hid = [Scatter(by_col, part.at[s], rbuf.at[s], r_ss.at[s], r_rs.at[s]) for s in halves]
    dx = [Scatter(by_row, inp.at[s], rbufx.at[s], r_ss.at[2 + s], r_rs.at[2 + s]) for s in halves]

    to_mate = [
        pltpu.make_async_remote_copy(
            pre_ref.at[:, units(1 - k)], pre_loc.at[k], k_ss.at[0], k_rs.at[0], mate, MESH),
        pltpu.make_async_remote_copy(w2_ref.at[units(1 - k)], w2.at[k], k_ss.at[1], k_rs.at[1], mate, MESH),
    ]

    def activate(f):
        def some(n, _):
            at = pl.ds(pl.multiple_of(f * W + n * 256, 256), 256)
            to = pl.ds(pl.multiple_of(n * 256, 256), 256)
            for s in halves:
                a = pre_loc[s, :, at].astype(F32)
                t = jnp.tanh(ROOT * (a + CUBE * (a * a * a)))
                act_all[k, f, s, mine_col, to] = (0.5 * a * (1.0 + t)).astype(BF)
                slope[s, :, at] = 0.5 * (1.0 + t) + 0.5 * a * (1.0 - t * t) * (ROOT * (1.0 + 3.0 * CUBE * (a * a)))
            return 0

        lax.fori_loop(0, W // 256, some, 0)

    def pre_grad(s):
        grad = hid[s].result().astype(BF).astype(F32)
        pre_all[k, s, mine_col] = (slope[s] * grad).astype(BF)

    def hidden(s, dg):
        at = pl.ds(pl.multiple_of(((y + dg) % 4) * 2 * T, 2 * T), 2 * T)

        for n in range(U // 256):
            to = pl.ds(n * 256, 256)
            part[s, at, to] = (dot(og_all[0, s, at], w2t[0, :, to]) + dot(og_all[1, s, at], w2t[1, :, to])).astype(BF)

    def input_part(s, dg):
        one, two = dx[s].at(dg, False), dx[s].at(dg, True)

        left = [jnp.concatenate([pre_all[core, s, one], pre_all[core, s, two]], axis=0) for core in (0, 1)]
        for n in range(W // 256):
            to = pl.ds(n * 256, 256)
            total = sum(dot(left[core], w1t[pl.ds(core * U, U), to]) for core in (0, 1)).astype(BF)
            inp[s, one, to] = total[:T]
            inp[s, two, to] = total[T:]

    def second_grad(n):
        at = pl.ds(n * W, W)
        total = sum(tl_dot(act_all[n // 2, n % 2, s], og_all[k, s]) for s in halves)
        out2[at] = total.astype(BF)

    def first_grad(n):
        at = pl.ds(n * W, W)
        total = sum(tl_dot(in_all[s], pre_all[n // 2, s, :, pl.ds((n % 2) * W, W)]) for s in halves)
        out1[:, at] = total.astype(BF)

    def input_grad(s):
        dxv[pl.ds(s * T, T)] = dx[s].result().astype(BF)

    og[0].start()
    to_mate[0].start()
    loads[0].wait()
    to_mate[0].wait_recv()
    activate(0)
    act[0].start()
    activate(1)
    act[1].start()
    to_mate[1].start()
    for load in loads[4:]:
        load.start()
    og[0].take(0, 1, 2)
    act[0].give_own()
    loads[3].wait()
    w2t[k] = w2[k].T
    og[0].take(4, 3)
    og[1].start()
    act[1].give_own()
    to_mate[1].wait_recv()
    w2t[1 - k] = w2[1 - k].T
    og[0].take(5, 6)
    act[0].take_near()
    act[0].give_near()
    loads[1].wait()
    og[0].take_mate()

    hidden(0, 2)
    hid[0].far()
    og[1].take(0, 1, 2)
    hidden(0, 1)
    hidden(0, 3)
    hid[0].near()
    act[1].take_near()
    act[0].take_far()
    og[1].take(4, 3)
    hidden(0, 0)
    og[1].take(5, 6)
    hid[0].fold()
    act[1].give_near()
    xs[0].start()
    act[0].take_pair(0, 1, 2)
    loads[2].wait()
    og[1].take_mate()
    hidden(1, 2)
    hid[1].far()
    hidden(1, 1)
    hidden(1, 3)
    hid[1].near()
    hidden(1, 0)
    act[1].take_far()
    hid[0].cross()
    xs[0].take(0, 1, 2)
    xs[1].start()
    hid[1].fold()
    pre_grad(0)
    pre[0].start()
    xs[0].take(4, 3)
    hid[1].cross()
    pre[0].take(0, 1, 2)
    xs[1].take(0, 1, 2)
    pre_grad(1)
    pre[1].start()
    pre[0].take(4, 3)
    xs[0].take(5, 6)
    xs[1].take(4, 3)
    loads[6].wait()
    w1t[...] = w1[...].T
    act[1].take_pair(0, 1, 2)
    pre[0].take(5, 6)
    pre[1].take(0, 1, 2)
    act[0].give_far()
    act[1].give_far()
    pre[0].take_mate()

    input_part(0, 2)
    dx[0].far()
    input_part(0, 1)
    input_part(0, 3)
    dx[0].near()
    pre[1].take(4, 3)
    input_part(0, 0)
    xs[1].take(5, 6)
    dx[0].fold()
    act[0].take_pair(3)
    act[1].take_pair(3)
    act[0].take_mate()
    second_grad(0)
    act[1].take_mate()
    second_grad(1)
    pre[1].take(5, 6)
    dx[0].cross()
    pre[1].take_mate()
    input_part(1, 2)
    dx[1].far()
    input_part(1, 1)
    input_part(1, 3)
    dx[1].near()
    input_part(1, 0)
    input_grad(0)
    loads[4].wait()
    loads[5].wait()
    first_grad(0)
    dx[1].fold()
    first_grad(1)
    first_grad(2)
    dx[1].cross()
    first_grad(3)
    second_grad(2)
    second_grad(3)
    input_grad(1)
    for item in (*og, *xs, *act, *pre, *hid, *dx):
        item.drain()
    for copy in to_mate:
        copy.wait_send()


def write_out(dx, dw1, dw2, dx_out, dw1_out, dw2_out, sems):
    copies = [
        pltpu.make_async_copy(src, dst, sems.at[i])
        for i, (src, dst) in enumerate(((dw1, dw1_out), (dw2, dw2_out), (dx, dx_out)))
    ]
    for copy in copies:
        copy.start()
    for copy in copies:
        copy.wait()


def local(inputs, pre_act, w_first, w_second, out_grad):
    sem = pltpu.SemaphoreType.DMA
    vm = lambda *shape, dtype=BF: pltpu.VMEM(shape, dtype)
    results = pl.pallas_call(
        kernel,
        out_shape=(
            pltpu.VMEM((2 * T, W), BF),
            pltpu.VMEM((W, 2 * U), BF),
            pltpu.VMEM((2 * U, W), BF),
        ),
        in_specs=[pl.BlockSpec(memory_space=pl.ANY)] * 5,
        out_specs=[pl.BlockSpec(memory_space=pltpu.VMEM)] * 3,
        scratch_shapes=[
            vm(2, 2, HALF, W),
            vm(2, HALF, W),
            vm(2, 2, 2, HALF, W),
            vm(2, 2, HALF, U),
            vm(2, T, U),
            vm(2, T, U, dtype=F32),
            vm(W, 2 * U),
            vm(2, U, W),
            vm(2, HALF, U),
            vm(2, HALF, W),
            vm(2, 7, T, U),
            vm(2, 7, T, W),
            vm(2 * U, W),
            vm(2, W, U),
            sem((8, 16)), sem((8, 16)), sem((4, 7)), sem((4, 7)), sem((2,)), sem((2,)), sem((7,)),
        ],
        compiler_params=pltpu.CompilerParams(
            collective_id=0, has_side_effects=True, vmem_limit_bytes=50 * 2**20
        ),
        cost_estimate=pl.CostEstimate(flops=19_327_352_832, bytes_accessed=20_000_000, transcendentals=400_000),
        name="ffn_back",
    )(inputs, pre_act, w_first, w_second, out_grad)
    return pl.pallas_call(
        write_out,
        out_shape=[jax.ShapeDtypeStruct(array.shape, BF) for array in results],
        in_specs=[pl.BlockSpec(memory_space=pltpu.VMEM)] * 3,
        out_specs=[pl.BlockSpec(memory_space=pl.ANY)] * 3,
        scratch_shapes=[sem((3,))],
        compiler_params=pltpu.CompilerParams(vmem_limit_bytes=1024 * 1024),
        name="write_out",
    )(*results)


def solution(mesh):
    placed = (P("row", "col"), P("col", "row"), P("col", "row"), P("row", "col"), P("row", "col"))
    return jax.shard_map(
        local,
        mesh=mesh,
        in_specs=placed,
        out_specs=(P("row", "col"), P("col", "row"), P("row", "col")),
        check_vma=False,
    )
```

```python
import jax
import jax.numpy as jnp
from jax import lax
from jax.experimental import pallas as pl
from jax.experimental.pallas import tpu as pltpu
from jax.sharding import PartitionSpec as P

MESH = pl.DeviceIdType.MESH
N = 1024
T = 128
PARTS = ((0, 48), (48, 48), (96, 32))
XPARTS = ((0, 64), (64, 64))
W = 768
U = 1536
F = 2
V = U // F
BF = jnp.bfloat16
F32 = jnp.float32
ROOT = 0.7978845608028654
CUBE = 0.044715


def dot(left, right):
    return jnp.dot(left, right, preferred_element_type=F32)


def tl_dot(left, right):
    return lax.dot_general(left, right, (((0,), (0,)), ((), ())), preferred_element_type=F32)


class Group:
    def __init__(self, g, h, device, block):
        self.g, self.h = g, h
        self.above, self.below, self.pair = device((g + 1) % 4, h), device((g + 3) % 4, h), device(g, 1 - h)
        self.block = lambda dg, other: block((g + dg) % 4, (1 - h) if other else h)


def span(group, owner, part):
    start, size = part
    return pl.ds(pl.multiple_of(group.block(*owner) * T + start, 16), size)


OWN, PAIR = (0, False), (0, True)
BELOW, ABOVE, FAR = (3, False), (1, False), (2, False)
PAIR_BELOW, PAIR_ABOVE, PAIR_FAR = (3, True), (1, True), (2, True)


class Gather:
    def __init__(self, group, part, buf, mate_buf, mate, ssem, rsem, own_src=None):
        self.group, self.part, self.buf, self.mate_buf, self.mate = group, part, buf, mate_buf, mate
        self.ssem, self.rsem, self.own_src = ssem, rsem, own_src
        self.sent = []

    def _ref(self, buf, owner, half=None):
        start, size = self.part
        if half is not None:
            start, size = start + half * (size // 2), size // 2
        return buf.at[span(self.group, owner, (start, size))]

    def _copy(self, slot, owner, device, half=None):
        ref = self._ref(self.buf, owner, half)
        own = owner == OWN and self.own_src is not None
        return pltpu.make_async_remote_copy(
            self.own_src if own else ref, ref, self.ssem.at[slot], self.rsem.at[slot], device, MESH)

    def _send(self, slot, owner, device, half=None):
        c = self._copy(slot, owner, device, half)
        c.start()
        self.sent.append(c)

    def _wait(self, slot, owner, half=None):
        self._copy(slot, owner, self.group.pair, half).wait_recv()

    def _take(self, slot, owner):
        self._wait(slot, owner)
        self._mate(owner)

    def _mate(self, owner):
        if self.mate is not None:
            self._send(8 + owner[0] * 2 + int(owner[1]), owner, self.mate)

    def give_mate(self):
        self._mate(OWN)

    def take_mate(self):
        for dg in range(4):
            for other in (False, True):
                ref, slot = self._ref(self.mate_buf, (dg, other)), 8 + dg * 2 + int(other)
                pltpu.make_async_remote_copy(
                    ref, ref, self.ssem.at[slot], self.rsem.at[slot], self.mate, MESH).wait_recv()

    def drain(self):
        for c in self.sent:
            c.wait_send()

    def send_own_up(self):
        self._send(0, OWN, self.group.above)

    def send_own_down(self):
        self._send(1, OWN, self.group.below)

    def send_own_pair(self):
        self._send(2, OWN, self.group.pair)

    def take_up(self):
        self._take(0, BELOW)

    def take_down(self):
        self._take(1, ABOVE)

    def take_pair(self):
        self._take(2, PAIR)

    def send_half_up(self):
        self._send(3, BELOW, self.group.above, 0)

    def send_half_down(self):
        self._send(4, ABOVE, self.group.below, 1)

    def take_far(self):
        self._wait(3, FAR, 0)
        self._wait(4, FAR, 1)
        self._mate(FAR)

    def send_pair_up(self):
        self._send(5, BELOW, self.group.pair)

    def send_pair_down(self):
        self._send(6, ABOVE, self.group.pair)

    def send_pair_far(self):
        self._send(7, FAR, self.group.pair)

    def take_pair_up(self):
        self._take(5, PAIR_BELOW)

    def take_pair_down(self):
        self._take(6, PAIR_ABOVE)

    def take_pair_far(self):
        self._take(7, PAIR_FAR)

    def send_other_up(self):
        self._send(5, PAIR, self.group.above)

    def send_other_down(self):
        self._send(6, PAIR, self.group.below)

    def take_other_up(self):
        self._take(5, PAIR_BELOW)

    def take_other_down(self):
        self._take(6, PAIR_ABOVE)

    def send_far_up(self):
        self._send(3, BELOW, self.group.above)

    def send_far_down(self):
        self._send(4, PAIR_ABOVE, self.group.below)

    def take_far_up(self):
        self._take(3, FAR)

    def take_far_down(self):
        self._take(4, PAIR_FAR)

    def start(self):
        self.send_own_pair()
        self.send_own_up()
        self.send_own_down()
        self.give_mate()

    def take(self, step):
        if step == 0:
            self._wait(2, PAIR)
            self.send_other_up()
            self.send_other_down()
            self._mate(PAIR)
        elif step == 1:
            self._wait(0, BELOW)
            self.send_far_up()
            self._mate(BELOW)
        elif step == 2:
            self.take_down()
        elif step == 3:
            self.take_other_up()
        elif step == 4:
            self._wait(6, PAIR_ABOVE)
            self.send_far_down()
            self._mate(PAIR_ABOVE)
        elif step == 5:
            self.take_far_up()
        else:
            self.take_far_down()


class Scatter:
    def __init__(self, group, part, terms, rbuf, ssem, rsem):
        self.group, self.part, self.terms, self.ssem, self.rsem = group, part, terms, ssem, rsem
        self.rbuf = rbuf.at[:, pl.ds(*part)]
        self.sent = []

    def at(self, dg, other):
        return span(self.group, (dg, other), self.part)

    def _copy(self, slot, at, device):
        return pltpu.make_async_remote_copy(
            self.terms.at[at], self.rbuf.at[slot], self.ssem.at[slot], self.rsem.at[slot], device, MESH)

    def _send(self, slot, dg, other, device):
        c = self._copy(slot, self.at(dg, other), device)
        c.start()
        self.sent.append(c)

    def _wait(self, slot):
        self._copy(slot, self.at(0, False), self.group.pair).wait_recv()

    def far(self):
        self._send(0, 2, False, self.group.above)
        self._send(1, 2, True, self.group.below)

    def near(self):
        self._send(2, 1, True, self.group.above)
        self._send(3, 3, False, self.group.below)

    def fold(self, way):
        dg, other, device = ((1, False, self.group.above), (3, True, self.group.below))[way]
        self._wait(way)
        at = self.at(dg, other)
        self.terms[at] = (self.terms[at].astype(F32) + self.rbuf[way].astype(F32)).astype(BF)
        self._send(way + 4, dg, other, device)

    def _total(self, other):
        direct, folded = (2, 5) if other else (3, 4)
        return (self.terms[self.at(0, other)].astype(F32) + self.rbuf[direct].astype(F32)
                + self.rbuf[folded].astype(F32))

    def cross(self):
        self._wait(2)
        self._wait(5)
        self.terms[self.at(0, True)] = self._total(True).astype(BF)
        self._send(6, 0, True, self.group.pair)

    def result(self):
        self._wait(3)
        self._wait(4)
        own = self._total(False)
        self._wait(6)
        return own + self.rbuf[6].astype(F32)

    def drain(self):
        for c in self.sent:
            c.wait_send()


def kernel(in_ref, pre_ref, w1_ref, w2_ref, og_ref, dxv, out1, out2,
           og_all, in_all, act_all, pre_all, pre_loc, slope, w1, w2, terms, inp, rbuf, rbufx, w1t, w2t,
           og_ss, og_rs, xs_ss, xs_rs, act_ss, act_rs, pre_ss, pre_rs, hid_ss, hid_rs, dx_ss, dx_rs, k_ss, k_rs, l_sem):
    r, c = lax.axis_index("row"), lax.axis_index("col")
    x, zl = r % 4, r // 4
    y, zh, k = c // 4, (c // 2) % 2, c % 2
    mate = (r, c + 1 - 2 * k)
    by_row = Group(x, zl, lambda g, h: (h * 4 + g, c), lambda g, h: h * 4 + g)
    by_col = Group(y, zh, lambda g, h: (r, g * 4 + h * 2 + k), lambda g, h: g * 2 + h)
    mine_row = span(by_row, OWN, (0, T))
    mine_col = span(by_col, OWN, (0, T))
    own64 = pl.ds(pl.multiple_of(k * (T // 2), T // 2), T // 2)

    def units(core):
        return pl.ds(pl.multiple_of(core * U, U), U)

    loads = [
        pltpu.make_async_copy(pre_ref.at[:, units(k)], pre_loc.at[own64], l_sem.at[0]),
        pltpu.make_async_copy(og_ref, og_all.at[k, mine_row], l_sem.at[1]),
        pltpu.make_async_copy(w2_ref.at[units(k)], w2.at[k], l_sem.at[2]),
        pltpu.make_async_copy(in_ref, in_all.at[mine_row], l_sem.at[3]),
        pltpu.make_async_copy(w1_ref, w1, l_sem.at[4]),
    ]
    for load in loads[:3]:
        load.start()

    barrier = pltpu.get_barrier_semaphore()
    friends = (mate, by_row.above, by_row.below, by_row.pair, by_col.above, by_col.below, by_col.pair)
    for friend in friends:
        pl.semaphore_signal(barrier, inc=1, device_id=friend, device_id_type=MESH)
    pl.semaphore_wait(barrier, len(friends))

    og = [Gather(by_row, part, og_all.at[k], og_all.at[1 - k], mate, og_ss.at[i], og_rs.at[i], og_ref.at[pl.ds(*part)])
          for i, part in enumerate(PARTS)]
    xs = [Gather(by_row, part, in_all, None, None, xs_ss.at[i], xs_rs.at[i], in_ref.at[pl.ds(*part)])
          for i, part in enumerate(XPARTS)]
    act = [Gather(by_col, (0, T), act_all.at[k, f], act_all.at[1 - k, f], mate, act_ss.at[f], act_rs.at[f])
           for f in range(F)]
    pre = [Gather(by_col, part, pre_all.at[k], pre_all.at[1 - k], mate, pre_ss.at[i], pre_rs.at[i])
           for i, part in enumerate(PARTS)]
    hid = [Scatter(by_col, part, terms, rbuf, hid_ss.at[i], hid_rs.at[i]) for i, part in enumerate(PARTS)]
    dx = [Scatter(by_row, part, inp, rbufx, dx_ss.at[i], dx_rs.at[i]) for i, part in enumerate(PARTS)]

    to_mate = [
        pltpu.make_async_remote_copy(
            pre_ref.at[:, units(1 - k)], pre_loc.at[own64], k_ss.at[0], k_rs.at[0], mate, MESH),
        pltpu.make_async_remote_copy(w2_ref.at[units(1 - k)], w2.at[k], k_ss.at[1], k_rs.at[1], mate, MESH),
    ]

    def activate(f):
        def some(n, _):
            at = pl.ds(pl.multiple_of(f * V + n * 128, 128), 128)
            to = pl.ds(pl.multiple_of(n * 128, 128), 128)
            a = pre_loc[:, at].astype(F32)
            t = jnp.tanh(ROOT * (a + CUBE * (a * a * a)))
            act_all[k, f, mine_col, to] = (0.5 * a * (1.0 + t)).astype(BF)
            slope[:, at] = 0.5 * (1.0 + t) + 0.5 * a * (1.0 - t * t) * (ROOT * (1.0 + 3.0 * CUBE * (a * a)))
            return 0

        lax.fori_loop(0, V // 128, some, 0)

    def pre_grad(s):
        grad = hid[s].result().astype(BF).astype(F32)
        pre_all[k, span(by_col, OWN, PARTS[s])] = (slope[pl.ds(*PARTS[s])] * grad).astype(BF)

    def blocks(scatter, dgs):
        return [scatter.at(dg, other) for dg in dgs for other in (False, True)]

    def product(scatter, dgs, lefts, rights, width, out):
        places, size = blocks(scatter, dgs), scatter.part[1]
        lefts = [jnp.concatenate([left[at] for at in places], axis=0) for left in lefts]
        for n in range(width // 256):
            to = pl.ds(n * 256, 256)
            total = sum(dot(left, right[:, to]) for left, right in zip(lefts, rights)).astype(BF)
            for i, at in enumerate(places):
                out[at, to] = total[i * size:(i + 1) * size]

    def hidden(s, *dgs):
        product(hid[s], dgs, [og_all.at[core] for core in (0, 1)], [w2t.at[core] for core in (0, 1)], U, terms)

    def input_part(s, *dgs):
        product(dx[s], dgs, [pre_all.at[core] for core in (0, 1)], [w1t.at[pl.ds(core * U, U)] for core in (0, 1)], W, inp)

    def second_grad(core, f):
        out2[pl.ds(core * U + f * V, V)] = tl_dot(act_all[core, f], og_all[k]).astype(BF)

    def first_grad(n):
        out1[:, pl.ds(n * W, W)] = tl_dot(in_all[...], pre_all[n // 2, :, pl.ds((n % 2) * W, W)]).astype(BF)

    def input_grad(s):
        dxv[pl.ds(*PARTS[s])] = dx[s].result().astype(BF)

    og[0].start()
    to_mate[0].start()
    loads[0].wait()
    to_mate[0].wait_recv()
    activate(0)
    act[0].send_own_down()
    act[0].send_own_up()
    for load in loads[3:]:
        load.start()
    act[0].send_own_pair()
    og[0].take(0)
    og[0].take(1)
    to_mate[1].start()
    activate(1)
    og[0].take(2)
    act[1].send_own_down()
    act[1].send_own_up()
    xs[0].send_own_up()
    og[0].take(4)
    og[1].start()
    og[0].take(5)
    xs[1].send_own_pair()
    act[0].take_pair()
    act[1].send_own_pair()
    act[0].take_up()
    act[0].take_down()
    act[0].send_half_down()
    og[0].take(3)
    og[0].take(6)
    loads[2].wait()
    w2t[k] = w2[k].T
    og[1].take(0)
    act[0].send_half_up()
    xs[0].take_up()
    to_mate[1].wait_recv()
    w2t[1 - k] = w2[1 - k].T
    act[1].take_down()
    act[1].send_half_down()
    act[1].take_up()
    act[1].send_half_up()
    xs[1].take_pair()
    og[0].take_mate()
    loads[1].wait()
    hidden(0, 2)
    hid[0].far()
    xs[0].send_own_pair()
    og[1].take(3)
    act[0].give_mate()
    og[1].take(1)
    og[1].take(4)
    og[2].start()
    hidden(0, 1, 3, 0)
    hid[0].near()
    act[1].send_pair_up()
    hid[0].fold(1)
    og[1].take(2)
    og[2].take(1)
    og[1].take(6)
    og[1].take(5)
    xs[0].take_pair()
    act[1].send_pair_down()
    hid[0].fold(0)
    og[2].take(0)
    og[1].take_mate()
    hidden(1, 2)
    hid[1].far()
    xs[0].send_far_up()
    xs[1].send_other_down()
    hidden(1, 1, 3, 0)
    hid[1].near()
    og[2].take(5)
    og[2].take(2)
    hid[0].cross()
    og[2].take(3)
    xs[0].send_other_up()
    og[2].take(4)
    xs[1].take_other_down()
    xs[1].send_other_up()
    xs[1].send_far_down()
    hid[1].fold(1)
    act[1].take_far()
    xs[0].send_other_down()
    act[0].send_pair_down()
    og[2].take(6)
    act[1].take_pair_down()
    xs[0].send_own_down()
    hid[1].fold(0)
    og[2].take_mate()
    hidden(2, 2)
    hid[2].far()
    hidden(2, 1, 3, 0)
    hid[2].near()
    pre_grad(0)
    pre[0].start()
    hid[1].cross()
    hid[2].fold(0)
    act[1].send_pair_far()
    pre[0].take(0)
    act[0].take_far()
    pre[0].take(2)
    act[1].take_pair()
    hid[2].fold(1)
    act[1].take_pair_up()
    xs[1].send_own_up()
    xs[1].take_far_down()
    xs[0].take_other_down()
    pre_grad(1)
    pre[1].start()
    xs[1].send_own_down()
    act[1].take_pair_far()
    act[0].take_pair_down()
    loads[4].wait()
    w1t[...] = w1[...].T
    act[1].give_mate()
    hid[2].cross()
    pre[0].take(1)
    xs[0].take_other_up()
    pre[0].take(4)
    pre[1].take(0)
    pre[1].take(1)
    pre_grad(2)
    pre[2].start()
    pre[0].take(3)
    act[1].take_mate()
    xs[0].send_far_down()
    act[0].send_pair_up()
    act[0].send_pair_far()
    second_grad(0, 1)
    pre[0].take(6)
    pre[0].take(5)
    second_grad(1, 1)
    xs[1].take_other_up()
    pre[1].take(4)
    pre[1].take(2)
    pre[2].take(0)
    pre[1].take(3)
    pre[0].take_mate()
    input_part(0, 2)
    dx[0].far()
    input_part(0, 1, 3, 0)
    dx[0].near()
    pre[2].take(2)
    xs[0].take_far_down()
    xs[0].take_down()
    pre[1].take(5)
    pre[1].take(6)
    dx[0].fold(0)
    act[0].take_pair_up()
    dx[0].fold(1)
    xs[1].take_up()
    xs[0].take_far_up()
    xs[1].take_down()
    pre[2].take(1)
    xs[1].send_far_up()
    pre[1].take_mate()
    pre[2].take(4)
    input_part(1, 2)
    dx[1].far()
    act[0].take_pair_far()
    input_part(1, 1, 3, 0)
    dx[1].near()
    act[0].take_mate()
    pre[2].take(3)
    pre[2].take(5)
    dx[0].cross()
    pre[2].take(6)
    dx[1].fold(1)
    second_grad(0, 0)
    pre[2].take_mate()
    loads[3].wait()
    input_part(2, 2)
    dx[2].far()
    input_part(2, 1, 3, 0)
    dx[2].near()
    xs[1].take_far_up()
    first_grad(0)
    dx[1].fold(0)
    dx[2].fold(1)
    dx[1].cross()
    second_grad(1, 0)
    first_grad(1)
    dx[2].fold(0)
    dx[2].cross()
    input_grad(0)
    first_grad(3)
    first_grad(2)
    input_grad(1)
    input_grad(2)
    for item in (*og, *xs, *act, *pre, *hid, *dx):
        item.drain()
    for copy in to_mate:
        copy.wait_send()


def write_out(dx, dw1, dw2, dx_out, dw1_out, dw2_out, sems):
    copies = [
        pltpu.make_async_copy(src, dst, sems.at[i])
        for i, (src, dst) in enumerate(((dw1, dw1_out), (dw2, dw2_out), (dx, dx_out)))
    ]
    for copy in copies:
        copy.start()
    for copy in copies:
        copy.wait()


def local(inputs, pre_act, w_first, w_second, out_grad):
    sem, S, X = pltpu.SemaphoreType.DMA, len(PARTS), len(XPARTS)
    vm = lambda *shape, dtype=BF: pltpu.VMEM(shape, dtype)
    results = pl.pallas_call(
        kernel,
        out_shape=(
            pltpu.VMEM((T, W), BF),
            pltpu.VMEM((W, 2 * U), BF),
            pltpu.VMEM((2 * U, W), BF),
        ),
        in_specs=[pl.BlockSpec(memory_space=pl.ANY)] * 5,
        out_specs=[pl.BlockSpec(memory_space=pltpu.VMEM)] * 3,
        scratch_shapes=[
            vm(2, N, W),
            vm(N, W),
            vm(2, F, N, V),
            vm(2, N, U),
            vm(T, U),
            vm(T, U, dtype=F32),
            vm(W, 2 * U),
            vm(2, U, W),
            vm(N, U),
            vm(N, W),
            vm(7, T, U),
            vm(7, T, W),
            vm(2 * U, W),
            vm(2, W, U),
            sem((S, 16)), sem((S, 16)), sem((X, 7)), sem((X, 7)), sem((F, 16)), sem((F, 16)), sem((S, 16)), sem((S, 16)),
            sem((S, 7)), sem((S, 7)), sem((S, 7)), sem((S, 7)), sem((2,)), sem((2,)), sem((5,)),
        ],
        compiler_params=pltpu.CompilerParams(
            collective_id=0, has_side_effects=True, vmem_limit_bytes=50 * 2**20
        ),
        cost_estimate=pl.CostEstimate(flops=19_327_352_832, bytes_accessed=20_000_000, transcendentals=400_000),
        name="ffn_back",
    )(inputs, pre_act, w_first, w_second, out_grad)
    return pl.pallas_call(
        write_out,
        out_shape=[jax.ShapeDtypeStruct(array.shape, BF) for array in results],
        in_specs=[pl.BlockSpec(memory_space=pltpu.VMEM)] * 3,
        out_specs=[pl.BlockSpec(memory_space=pl.ANY)] * 3,
        scratch_shapes=[sem((3,))],
        compiler_params=pltpu.CompilerParams(vmem_limit_bytes=1024 * 1024),
        name="write_out",
    )(*results)


def solution(mesh):
    placed = (P("row", "col"), P("col", "row"), P("col", "row"), P("row", "col"), P("row", "col"))
    return jax.shard_map(
        local,
        mesh=mesh,
        in_specs=placed,
        out_specs=(P("row", "col"), P("col", "row"), P("row", "col")),
        check_vma=False,
    )
```

```python
import jax
import jax.numpy as jnp
from jax import lax
from jax.experimental import pallas as pl
from jax.experimental.pallas import tpu as pltpu
from jax.sharding import PartitionSpec as P

MESH = pl.DeviceIdType.MESH
N = 1024
T = 128
PARTS = ((0, 48), (48, 48), (96, 32))
XPARTS = ((0, 64), (64, 64))
W = 768
U = 1536
F = 4
V = U // F
BF = jnp.bfloat16
F32 = jnp.float32
ROOT = 0.7978845608028654
CUBE = 0.044715


def dot(left, right):
    return jnp.dot(left, right, preferred_element_type=F32)


def tl_dot(left, right):
    return lax.dot_general(left, right, (((0,), (0,)), ((), ())), preferred_element_type=F32)


class Group:
    def __init__(self, g, h, device, block):
        self.g, self.h = g, h
        self.above, self.below, self.pair = device((g + 1) % 4, h), device((g + 3) % 4, h), device(g, 1 - h)
        self.block = lambda dg, other: block((g + dg) % 4, (1 - h) if other else h)
        self.device = lambda dg, other: device((g + dg) % 4, (1 - h) if other else h)


def span(group, owner, part):
    start, size = part
    return pl.ds(pl.multiple_of(group.block(*owner) * T + start, 16), size)


OWN, PAIR = (0, False), (0, True)
BELOW, ABOVE, FAR = (3, False), (1, False), (2, False)
PAIR_BELOW, PAIR_ABOVE, PAIR_FAR = (3, True), (1, True), (2, True)
OTHERS = (FAR, PAIR_FAR, PAIR, BELOW, ABOVE, PAIR_BELOW, PAIR_ABOVE)


def seen_from(place):
    return (4 - place[0]) % 4, place[1]


class Gather:
    def __init__(self, group, part, buf, mate_buf, mate, ssem, rsem, own_src=None, core=0):
        self.group, self.part, self.buf, self.mate_buf, self.mate = group, part, buf, mate_buf, mate
        self.ssem, self.rsem, self.own_src, self.core = ssem, rsem, own_src, core
        self.sent = []

    def _ref(self, buf, owner, half=None):
        start, size = self.part
        if half is not None:
            start, size = start + half * (size // 2), size // 2
        return buf.at[span(self.group, owner, (start, size))]

    def _copy(self, slot, owner, device, half=None):
        ref = self._ref(self.buf, owner, half)
        own = owner == OWN and self.own_src is not None
        return pltpu.make_async_remote_copy(
            self.own_src if own else ref, ref, self.ssem.at[slot], self.rsem.at[slot], device, MESH)

    def _send(self, slot, owner, device, half=None):
        c = self._copy(slot, owner, device, half)
        c.start()
        self.sent.append(c)

    def _wait(self, slot, owner, half=None):
        self._copy(slot, owner, self.group.pair, half).wait_recv()

    def _take(self, slot, owner):
        self._wait(slot, owner)
        self._mate(owner)

    def _mate(self, owner):
        if self.mate is not None:
            self._send(8 + owner[0] * 2 + int(owner[1]), owner, self.mate)

    def give_mate(self):
        self._mate(OWN)

    def take_mate(self):
        for dg in range(4):
            for other in (False, True):
                ref, slot = self._ref(self.mate_buf, (dg, other)), 8 + dg * 2 + int(other)
                pltpu.make_async_remote_copy(
                    ref, ref, self.ssem.at[slot], self.rsem.at[slot], self.mate, MESH).wait_recv()

    def drain(self):
        for c in self.sent:
            c.wait_send()

    def send_own_up(self):
        self._send(0, OWN, self.group.above)

    def send_own_down(self):
        self._send(1, OWN, self.group.below)

    def send_own_pair(self):
        self._send(2, OWN, self.group.pair)

    def take_up(self):
        self._take(0, BELOW)

    def take_down(self):
        self._take(1, ABOVE)

    def take_pair(self):
        self._take(2, PAIR)

    def send_half_up(self):
        self._send(3, BELOW, self.group.above, 0)

    def send_half_down(self):
        self._send(4, ABOVE, self.group.below, 1)

    def take_far(self):
        self._wait(3, FAR, 0)
        self._wait(4, FAR, 1)
        self._mate(FAR)

    def send_pair_up(self):
        self._send(5, BELOW, self.group.pair)

    def send_pair_down(self):
        self._send(6, ABOVE, self.group.pair)

    def send_pair_far(self):
        self._send(7, FAR, self.group.pair)

    def take_pair_up(self):
        self._take(5, PAIR_BELOW)

    def take_pair_down(self):
        self._take(6, PAIR_ABOVE)

    def take_pair_far(self):
        self._take(7, PAIR_FAR)

    def send_other_up(self):
        self._send(5, PAIR, self.group.above)

    def send_other_down(self):
        self._send(6, PAIR, self.group.below)

    def take_other_up(self):
        self._take(5, PAIR_BELOW)

    def take_other_down(self):
        self._take(6, PAIR_ABOVE)

    def send_far_up(self):
        self._send(3, BELOW, self.group.above)

    def send_far_down(self):
        self._send(4, PAIR_ABOVE, self.group.below)

    def take_far_up(self):
        self._take(3, FAR)

    def take_far_down(self):
        self._take(4, PAIR_FAR)

    def start_direct(self):
        for place in OTHERS:
            self._send(OTHERS.index(seen_from(place)), OWN, self.group.device(*place))
        self.give_mate()

    def take_direct(self, step):
        owner = (PAIR, BELOW, ABOVE, PAIR_BELOW, PAIR_ABOVE, FAR, PAIR_FAR)[step]
        self._take(OTHERS.index(owner), owner)

    def _send_rows(self, slot, device, core):
        at = self._rows(OWN, core)
        c = pltpu.make_async_remote_copy(
            self.buf.at[at], self.buf.at[at], self.ssem.at[slot], self.rsem.at[slot], device, MESH)
        c.start()
        self.sent.append(c)

    def _rows(self, owner, core):
        return pl.ds(pl.multiple_of(self.group.block(*owner) * T + core * (T // 2), T // 2), T // 2)

    def _take_rows(self, slots, owner):
        for slot, core in zip(slots, (self.core, 1 - self.core)):
            ref = self.buf.at[self._rows(owner, core)]
            pltpu.make_async_remote_copy(
                ref, ref, self.ssem.at[slot], self.rsem.at[slot], self.group.pair, MESH).wait_recv()
        self._mate(owner)

    def send_mine_up(self):
        self._send_rows(0, self.group.above, self.core)

    def send_mine_down(self):
        self._send_rows(1, self.group.below, self.core)

    def send_mates_up(self):
        self._send_rows(16, self.group.above, 1 - self.core)

    def send_mates_down(self):
        self._send_rows(17, self.group.below, 1 - self.core)

    def take_up2(self):
        self._take_rows((0, 16), BELOW)

    def take_down2(self):
        self._take_rows((1, 17), ABOVE)

    def start(self):
        self.send_own_pair()
        self.send_own_up()
        self.send_own_down()
        self.give_mate()

    def take(self, step):
        if step == 0:
            self._wait(2, PAIR)
            self.send_other_up()
            self.send_other_down()
            self._mate(PAIR)
        elif step == 1:
            self._wait(0, BELOW)
            self.send_far_up()
            self._mate(BELOW)
        elif step == 2:
            self.take_down()
        elif step == 3:
            self.take_other_up()
        elif step == 4:
            self._wait(6, PAIR_ABOVE)
            self.send_far_down()
            self._mate(PAIR_ABOVE)
        elif step == 5:
            self.take_far_up()
        else:
            self.take_far_down()


class Scatter:
    def __init__(self, group, part, terms, rbuf, ssem, rsem):
        self.group, self.part, self.terms, self.ssem, self.rsem = group, part, terms, ssem, rsem
        self.rbuf = rbuf.at[:, pl.ds(*part)]
        self.sent = []

    def at(self, dg, other):
        return span(self.group, (dg, other), self.part)

    def _copy(self, slot, at, device):
        return pltpu.make_async_remote_copy(
            self.terms.at[at], self.rbuf.at[slot], self.ssem.at[slot], self.rsem.at[slot], device, MESH)

    def _send(self, slot, dg, other, device):
        c = self._copy(slot, self.at(dg, other), device)
        c.start()
        self.sent.append(c)

    def _wait(self, slot):
        self._copy(slot, self.at(0, False), self.group.pair).wait_recv()

    def direct(self, *dgs):
        for place in OTHERS + (OWN,):
            if place[0] in dgs and place != OWN:
                self._send(OTHERS.index(seen_from(place)), *place, self.group.device(*place))

    def result_direct(self):
        for slot in range(7):
            self._wait(slot)
        return self.terms[self.at(*OWN)].astype(F32) + sum(self.rbuf[slot].astype(F32) for slot in range(7))

    def far(self):
        self._send(0, 2, False, self.group.above)
        self._send(1, 2, True, self.group.below)

    def near(self):
        self._send(2, 1, True, self.group.above)
        self._send(3, 3, False, self.group.below)

    def fold(self, way):
        dg, other, device = ((1, False, self.group.above), (3, True, self.group.below))[way]
        self._wait(way)
        at = self.at(dg, other)
        self.terms[at] = (self.terms[at].astype(F32) + self.rbuf[way].astype(F32)).astype(BF)
        self._send(way + 4, dg, other, device)

    def _total(self, other):
        direct, folded = (2, 5) if other else (3, 4)
        return (self.terms[self.at(0, other)].astype(F32) + self.rbuf[direct].astype(F32)
                + self.rbuf[folded].astype(F32))

    def cross(self):
        self._wait(2)
        self._wait(5)
        self.terms[self.at(0, True)] = self._total(True).astype(BF)
        self._send(6, 0, True, self.group.pair)

    def result(self):
        self._wait(3)
        self._wait(4)
        own = self._total(False)
        self._wait(6)
        return own + self.rbuf[6].astype(F32)

    def drain(self):
        for c in self.sent:
            c.wait_send()


def kernel(in_ref, pre_ref, w1_ref, w2_ref, og_ref, dxv, out1, out2,
           og_all, in_all, act_all, pre_all, pre_loc, slope, w1, w2, terms, inp, rbuf, rbufx, w1t, w2t,
           og_ss, og_rs, xs_ss, xs_rs, act_ss, act_rs, pre_ss, pre_rs, hid_ss, hid_rs, dx_ss, dx_rs, k_ss, k_rs, l_sem):
    r, c = lax.axis_index("row"), lax.axis_index("col")
    x, zl = r % 4, r // 4
    y, zh, k = c // 4, (c // 2) % 2, c % 2
    mate = (r, c + 1 - 2 * k)
    by_row = Group(x, zl, lambda g, h: (h * 4 + g, c), lambda g, h: h * 4 + g)
    by_col = Group(y, zh, lambda g, h: (r, g * 4 + h * 2 + k), lambda g, h: g * 2 + h)
    mine_row = span(by_row, OWN, (0, T))
    mine_col = span(by_col, OWN, (0, T))
    own64 = pl.ds(pl.multiple_of(k * (T // 2), T // 2), T // 2)

    def units(core):
        return pl.ds(pl.multiple_of(core * U, U), U)

    loads = [
        pltpu.make_async_copy(pre_ref.at[:, units(k)], pre_loc.at[own64], l_sem.at[0]),
        pltpu.make_async_copy(og_ref, og_all.at[k, mine_row], l_sem.at[1]),
        pltpu.make_async_copy(w2_ref.at[units(k)], w2.at[k], l_sem.at[2]),
        pltpu.make_async_copy(in_ref, in_all.at[mine_row], l_sem.at[3]),
        pltpu.make_async_copy(w1_ref, w1, l_sem.at[4]),
    ]
    for load in loads[:3]:
        load.start()

    barrier = pltpu.get_barrier_semaphore()
    friends = (mate, by_col.above, by_col.below, by_col.pair) + tuple(by_row.device(*place) for place in OTHERS)
    for friend in friends:
        pl.semaphore_signal(barrier, inc=1, device_id=friend, device_id_type=MESH)
    og = [Gather(by_row, part, og_all.at[k], og_all.at[1 - k], mate, og_ss.at[i], og_rs.at[i], og_ref.at[pl.ds(*part)])
          for i, part in enumerate(PARTS)]
    xs = [Gather(by_row, part, in_all, None, None, xs_ss.at[i], xs_rs.at[i], in_ref.at[pl.ds(*part)])
          for i, part in enumerate(XPARTS)]
    act = [Gather(by_col, (0, T), act_all.at[k, f], act_all.at[1 - k, f], mate, act_ss.at[f], act_rs.at[f],
                  core=k)
           for f in range(F)]
    pre = [Gather(by_col, part, pre_all.at[k], pre_all.at[1 - k], mate, pre_ss.at[i], pre_rs.at[i])
           for i, part in enumerate(PARTS)]
    hid = [Scatter(by_col, part, terms, rbuf, hid_ss.at[i], hid_rs.at[i]) for i, part in enumerate(PARTS)]
    dx = [Scatter(by_row, part, inp, rbufx, dx_ss.at[i], dx_rs.at[i]) for i, part in enumerate(PARTS)]

    to_mate = [
        pltpu.make_async_remote_copy(
            pre_ref.at[:, units(1 - k)], pre_loc.at[own64], k_ss.at[0], k_rs.at[0], mate, MESH),
        pltpu.make_async_remote_copy(w2_ref.at[units(1 - k)], w2.at[k], k_ss.at[1], k_rs.at[1], mate, MESH),
    ]

    def activate(f, core):
        tokens = pl.ds(pl.multiple_of(core * (T // 2), T // 2), T // 2)
        own = act[f]._rows(OWN, core)

        def some(n, _):
            at = pl.ds(pl.multiple_of(f * V + n * 128, 128), 128)
            to = pl.ds(pl.multiple_of(n * 128, 128), 128)
            a = pre_loc[tokens, at].astype(F32)
            t = jnp.tanh(ROOT * (a + CUBE * (a * a * a)))
            act_all[k, f, own, to] = (0.5 * a * (1.0 + t)).astype(BF)
            slope[tokens, at] = 0.5 * (1.0 + t) + 0.5 * a * (1.0 - t * t) * (ROOT * (1.0 + 3.0 * CUBE * (a * a)))
            return 0

        lax.fori_loop(0, V // 128, some, 0)

    def pre_grad(s):
        grad = hid[s].result().astype(BF).astype(F32)
        pre_all[k, span(by_col, OWN, PARTS[s])] = (slope[pl.ds(*PARTS[s])] * grad).astype(BF)

    def blocks(scatter, dgs):
        return [scatter.at(dg, other) for dg in dgs for other in (False, True)]

    def product(scatter, dgs, lefts, rights, width, out):
        places, size = blocks(scatter, dgs), scatter.part[1]
        lefts = [jnp.concatenate([left[at] for at in places], axis=0) for left in lefts]
        for n in range(width // 256):
            to = pl.ds(n * 256, 256)
            total = sum(dot(left, right[:, to]) for left, right in zip(lefts, rights)).astype(BF)
            for i, at in enumerate(places):
                out[at, to] = total[i * size:(i + 1) * size]

    def hidden(s, *dgs):
        product(hid[s], dgs, [og_all.at[core] for core in (0, 1)], [w2t.at[core] for core in (0, 1)], U, terms)

    def input_part(s, *dgs):
        product(dx[s], dgs, [pre_all.at[core] for core in (0, 1)], [w1t.at[pl.ds(core * U, U)] for core in (0, 1)], W, inp)

    def second_grad(core, f):
        out2[pl.ds(core * U + f * V, V)] = tl_dot(act_all[core, f], og_all[k]).astype(BF)

    def first_grad(n):
        out1[:, pl.ds(n * W, W)] = tl_dot(in_all[...], pre_all[n // 2, :, pl.ds((n % 2) * W, W)]).astype(BF)

    def input_grad(s, direct=False):
        dxv[pl.ds(*PARTS[s])] = (dx[s].result_direct() if direct else dx[s].result()).astype(BF)

    loads[0].wait()
    for f in range(F):
        activate(f, k)
    pl.semaphore_wait(barrier, len(friends))

    to_mate[0].start()
    act[3].send_mine_down()
    og[0].start_direct()
    act[0].send_mine_up()
    act[1].send_mine_down()
    to_mate[0].wait_recv()
    activate(0, 1 - k)
    to_mate[1].start()
    act[0].send_mates_up()
    activate(1, 1 - k)
    act[2].send_mine_down()
    act[1].send_mates_down()
    activate(2, 1 - k)
    act[2].send_mates_up()
    for load in loads[3:]:
        load.start()
    activate(3, 1 - k)
    act[0].send_mine_down()
    og[1].start()
    act[1].send_mine_up()
    loads[2].wait()
    w2t[k] = w2[k].T
    og[0].take_direct(0)
    act[3].send_mates_down()
    act[0].send_mates_down()
    act[1].send_mates_up()
    act[0].send_own_pair()
    act[0].take_up2()
    act[3].send_mates_up()
    act[2].send_mates_down()
    act[1].take_down2()
    og[0].take_direct(6)
    xs[0].send_own_pair()
    xs[1].send_own_pair()
    og[0].take_direct(5)
    act[3].send_mine_up()
    to_mate[1].wait_recv()
    w2t[1 - k] = w2[1 - k].T
    og[0].take_direct(2)
    act[0].send_half_up()
    xs[1].send_own_up()
    act[1].send_half_down()
    og[0].take_direct(1)
    act[1].take_up2()
    act[2].send_mine_up()
    act[3].take_down2()
    act[1].send_half_up()
    og[0].take_direct(3)
    og[0].take_direct(4)
    act[0].take_down2()
    act[1].send_own_pair()
    act[3].send_half_down()
    act[0].send_half_down()
    og[1].take(0)
    og[0].take_mate()
    loads[1].wait()
    hidden(0, 2)
    hid[0].far()
    hidden(0, 1, 3, 0)
    hid[0].near()
    og[1].take(4)
    og[1].take(1)
    og[1].take(3)
    og[2].start()
    act[0].send_pair_up()
    hid[0].fold(1)
    act[0].send_pair_down()
    xs[1].take_up()
    hid[0].fold(0)
    og[1].take(6)
    act[1].send_pair_up()
    og[1].take(5)
    xs[0].take_pair()
    og[1].take(2)
    xs[1].take_pair()
    act[0].take_far()
    og[2].take(1)
    og[2].take(0)
    og[1].take_mate()
    hidden(1, 2)
    hid[1].far()
    loads[4].wait()
    w1t[...] = w1[...].T
    act[3].take_up2()
    hidden(1, 1, 3, 0)
    hid[1].near()
    hid[0].cross()
    xs[1].send_other_down()
    og[2].take(4)
    og[2].take(3)
    act[3].send_pair_down()
    act[0].send_pair_far()
    og[2].take(5)
    act[3].send_half_up()
    xs[0].send_other_down()
    hid[1].fold(1)
    hid[1].fold(0)
    og[2].take(6)
    act[1].give_mate()
    pre_grad(0)
    pre[0].start()
    og[2].take(2)
    og[2].take_mate()
    act[0].give_mate()
    hidden(2, 2)
    hid[2].far()
    hid[1].cross()
    hidden(2, 1, 3, 0)
    hid[2].near()
    act[0].take_pair_up()
    act[3].give_mate()
    act[1].take_pair_up()
    act[1].send_pair_down()
    pre[0].take(0)
    xs[1].send_far_up()
    act[1].take_pair()
    loads[3].wait()
    xs[0].send_own_up()
    act[1].take_far()
    hid[2].fold(1)
    xs[1].send_own_down()
    act[0].take_pair_down()
    act[2].take_down2()
    act[2].take_up2()
    act[0].take_pair()
    act[3].send_own_pair()
    act[3].send_pair_up()
    act[3].take_far()
    pre[0].take(2)
    pre[0].take(1)
    xs[0].send_other_up()
    hid[2].fold(0)
    act[0].take_pair_far()
    pre[0].take(4)
    act[0].take_mate()
    pre_grad(1)
    pre[1].start()
    act[2].give_mate()
    second_grad(0, 0)
    second_grad(1, 0)
    xs[0].take_other_up()
    hid[2].cross()
    xs[0].take_up()
    pre[0].take(3)
    xs[1].send_other_up()
    act[1].send_pair_far()
    xs[1].take_other_down()
    xs[1].send_far_down()
    pre[0].take(5)
    pre[0].take(6)
    act[3].take_pair_down()
    xs[0].take_other_down()
    act[1].take_pair_down()
    act[3].send_pair_far()
    pre[1].take(0)
    xs[1].take_other_up()
    xs[0].send_far_down()
    xs[0].send_far_up()
    pre[0].take_mate()
    input_part(0, 2)
    dx[0].far()
    pre_grad(2)
    pre[2].start()
    pre[1].take(2)
    input_part(0, 1, 3, 0)
    dx[0].near()
    act[1].take_pair_far()
    pre[1].take(1)
    pre[1].take(4)
    xs[1].take_far_up()
    xs[1].take_far_down()
    xs[0].send_own_down()
    act[3].take_pair_up()
    act[2].send_own_pair()
    xs[0].take_far_down()
    act[3].take_pair()
    act[1].take_mate()
    second_grad(1, 1)
    act[3].take_pair_far()
    dx[0].fold(1)
    pre[1].take(3)
    act[2].send_pair_up()
    pre[2].take(0)
    pre[2].take(1)
    act[2].send_half_up()
    pre[2].take(2)
    second_grad(0, 1)
    dx[0].fold(0)
    act[3].take_mate()
    xs[0].take_far_up()
    pre[1].take(6)
    act[2].send_pair_down()
    act[2].send_half_down()
    pre[1].take(5)
    xs[0].take_down()
    second_grad(1, 3)
    act[2].take_pair()
    pre[2].take(4)
    dx[0].cross()
    xs[1].take_down()
    act[2].take_pair_up()
    pre[1].take_mate()
    input_part(1, 2)
    dx[1].far()
    pre[2].take(3)
    act[2].take_pair_down()
    input_part(1, 1, 3, 0)
    dx[1].near()
    pre[2].take(5)
    input_grad(0)
    pre[2].take(6)
    second_grad(0, 3)
    act[2].take_far()
    act[2].send_pair_far()
    dx[1].fold(0)
    dx[1].fold(1)
    pre[2].take_mate()
    input_part(2, 2)
    dx[2].direct(2)
    input_part(2, 1, 3, 0)
    dx[2].direct(1, 3, 0)
    first_grad(3)
    dx[1].cross()
    act[2].take_pair_far()
    first_grad(0)
    first_grad(2)
    act[2].take_mate()
    second_grad(0, 2)
    second_grad(1, 2)
    first_grad(1)
    input_grad(2, True)
    input_grad(1)
    for item in (*og, *xs, *act, *pre, *hid, *dx):
        item.drain()
    for copy in to_mate:
        copy.wait_send()


def write_out(dx, dw1, dw2, dx_out, dw1_out, dw2_out, sems):
    copies = [
        pltpu.make_async_copy(src, dst, sems.at[i])
        for i, (src, dst) in enumerate(((dw1, dw1_out), (dw2, dw2_out), (dx, dx_out)))
    ]
    for copy in copies:
        copy.start()
    for copy in copies:
        copy.wait()


def local(inputs, pre_act, w_first, w_second, out_grad):
    sem, S, X = pltpu.SemaphoreType.DMA, len(PARTS), len(XPARTS)
    vm = lambda *shape, dtype=BF: pltpu.VMEM(shape, dtype)
    results = pl.pallas_call(
        kernel,
        out_shape=(
            pltpu.VMEM((T, W), BF),
            pltpu.VMEM((W, 2 * U), BF),
            pltpu.VMEM((2 * U, W), BF),
        ),
        in_specs=[pl.BlockSpec(memory_space=pl.ANY)] * 5,
        out_specs=[pl.BlockSpec(memory_space=pltpu.VMEM)] * 3,
        scratch_shapes=[
            vm(2, N, W),
            vm(N, W),
            vm(2, F, N, V),
            vm(2, N, U),
            vm(T, U),
            vm(T, U, dtype=F32),
            vm(W, 2 * U),
            vm(2, U, W),
            vm(N, U),
            vm(N, W),
            vm(7, T, U),
            vm(7, T, W),
            vm(2 * U, W),
            vm(2, W, U),
            sem((S, 16)), sem((S, 16)), sem((X, 7)), sem((X, 7)), sem((F, 18)), sem((F, 18)), sem((S, 16)), sem((S, 16)),
            sem((S, 7)), sem((S, 7)), sem((S, 7)), sem((S, 7)), sem((2,)), sem((2,)), sem((5,)),
        ],
        compiler_params=pltpu.CompilerParams(
            collective_id=0, has_side_effects=True, vmem_limit_bytes=50 * 2**20
        ),
        cost_estimate=pl.CostEstimate(flops=19_327_352_832, bytes_accessed=20_000_000, transcendentals=400_000),
        name="ffn_back",
    )(inputs, pre_act, w_first, w_second, out_grad)
    return pl.pallas_call(
        write_out,
        out_shape=[jax.ShapeDtypeStruct(array.shape, BF) for array in results],
        in_specs=[pl.BlockSpec(memory_space=pltpu.VMEM)] * 3,
        out_specs=[pl.BlockSpec(memory_space=pl.ANY)] * 3,
        scratch_shapes=[sem((3,))],
        compiler_params=pltpu.CompilerParams(vmem_limit_bytes=1024 * 1024),
        name="write_out",
    )(*results)


def solution(mesh):
    placed = (P("row", "col"), P("col", "row"), P("col", "row"), P("row", "col"), P("row", "col"))
    return jax.shard_map(
        local,
        mesh=mesh,
        in_specs=placed,
        out_specs=(P("row", "col"), P("col", "row"), P("row", "col")),
        check_vma=False,
    )
```

```python
import jax
import jax.numpy as jnp
from jax import lax
from jax.experimental import pallas as pl
from jax.experimental.pallas import tpu as pltpu
from jax.sharding import PartitionSpec as P

MESH = pl.DeviceIdType.MESH
N = 1024
T = 128
PARTS = ((0, 48), (48, 48), (96, 32))
XPARTS = ((0, 64), (64, 64))
W = 768
U = 1536
F = 4
V = U // F
BF = jnp.bfloat16
F32 = jnp.float32
ROOT = 0.7978845608028654
CUBE = 0.044715


def dot(left, right):
    return jnp.dot(left, right, preferred_element_type=F32)


def tl_dot(left, right):
    return lax.dot_general(left, right, (((0,), (0,)), ((), ())), preferred_element_type=F32)


class Group:
    def __init__(self, g, h, device, block):
        self.g, self.h = g, h
        self.above, self.below, self.pair = device((g + 1) % 4, h), device((g + 3) % 4, h), device(g, 1 - h)
        self.block = lambda dg, other: block((g + dg) % 4, (1 - h) if other else h)
        self.device = lambda dg, other: device((g + dg) % 4, (1 - h) if other else h)


def span(group, owner, part):
    start, size = part
    return pl.ds(pl.multiple_of(group.block(*owner) * T + start, 16), size)


OWN, PAIR = (0, False), (0, True)
BELOW, ABOVE, FAR = (3, False), (1, False), (2, False)
PAIR_BELOW, PAIR_ABOVE, PAIR_FAR = (3, True), (1, True), (2, True)
OTHERS = (FAR, PAIR_FAR, PAIR, BELOW, ABOVE, PAIR_BELOW, PAIR_ABOVE)


def seen_from(place):
    return (4 - place[0]) % 4, place[1]


class Gather:
    def __init__(self, group, part, buf, mate_buf, mate, ssem, rsem, own_src=None, core=0):
        self.group, self.part, self.buf, self.mate_buf, self.mate = group, part, buf, mate_buf, mate
        self.ssem, self.rsem, self.own_src, self.core = ssem, rsem, own_src, core
        self.sent = []

    def _ref(self, buf, owner, half=None):
        start, size = self.part
        if half is not None:
            start, size = start + half * (size // 2), size // 2
        return buf.at[span(self.group, owner, (start, size))]

    def _copy(self, slot, owner, device, half=None):
        ref = self._ref(self.buf, owner, half)
        own = owner == OWN and self.own_src is not None
        return pltpu.make_async_remote_copy(
            self.own_src if own else ref, ref, self.ssem.at[slot], self.rsem.at[slot], device, MESH)

    def _send(self, slot, owner, device, half=None):
        c = self._copy(slot, owner, device, half)
        c.start()
        self.sent.append(c)

    def _wait(self, slot, owner, half=None):
        self._copy(slot, owner, self.group.pair, half).wait_recv()

    def _take(self, slot, owner):
        self._wait(slot, owner)
        self._mate(owner)

    def _mate(self, owner):
        if self.mate is not None:
            self._send(8 + owner[0] * 2 + int(owner[1]), owner, self.mate)

    def give_mate(self):
        self._mate(OWN)

    def take_mate(self):
        for dg in range(4):
            for other in (False, True):
                ref, slot = self._ref(self.mate_buf, (dg, other)), 8 + dg * 2 + int(other)
                pltpu.make_async_remote_copy(
                    ref, ref, self.ssem.at[slot], self.rsem.at[slot], self.mate, MESH).wait_recv()

    def drain(self):
        for c in self.sent:
            c.wait_send()

    def send_own_up(self):
        self._send(0, OWN, self.group.above)

    def send_own_down(self):
        self._send(1, OWN, self.group.below)

    def send_own_pair(self):
        self._send(2, OWN, self.group.pair)

    def take_up(self):
        self._take(0, BELOW)

    def take_down(self):
        self._take(1, ABOVE)

    def take_pair(self):
        self._take(2, PAIR)

    def send_half_up(self):
        self._send(3, BELOW, self.group.above, 0)

    def send_half_down(self):
        self._send(4, ABOVE, self.group.below, 1)

    def take_far(self):
        self._wait(3, FAR, 0)
        self._wait(4, FAR, 1)
        self._mate(FAR)

    def send_pair_up(self):
        self._send(5, BELOW, self.group.pair)

    def send_pair_down(self):
        self._send(6, ABOVE, self.group.pair)

    def send_pair_far(self):
        self._send(7, FAR, self.group.pair)

    def take_pair_up(self):
        self._take(5, PAIR_BELOW)

    def take_pair_down(self):
        self._take(6, PAIR_ABOVE)

    def take_pair_far(self):
        self._take(7, PAIR_FAR)

    def send_other_up(self):
        self._send(5, PAIR, self.group.above)

    def send_other_down(self):
        self._send(6, PAIR, self.group.below)

    def take_other_up(self):
        self._take(5, PAIR_BELOW)

    def take_other_down(self):
        self._take(6, PAIR_ABOVE)

    def send_far_up(self):
        self._send(3, BELOW, self.group.above)

    def send_far_down(self):
        self._send(4, PAIR_ABOVE, self.group.below)

    def take_far_up(self):
        self._take(3, FAR)

    def take_far_down(self):
        self._take(4, PAIR_FAR)

    def start_direct(self):
        for place in OTHERS:
            self._send(OTHERS.index(seen_from(place)), OWN, self.group.device(*place))
        self.give_mate()

    def take_direct(self, step):
        owner = (PAIR, BELOW, ABOVE, PAIR_BELOW, PAIR_ABOVE, FAR, PAIR_FAR)[step]
        self._take(OTHERS.index(owner), owner)

    def _send_rows(self, slot, device, core):
        at = self._rows(OWN, core)
        c = pltpu.make_async_remote_copy(
            self.buf.at[at], self.buf.at[at], self.ssem.at[slot], self.rsem.at[slot], device, MESH)
        c.start()
        self.sent.append(c)

    def _rows(self, owner, core):
        return pl.ds(pl.multiple_of(self.group.block(*owner) * T + core * (T // 2), T // 2), T // 2)

    def _take_rows(self, slots, owner):
        for slot, core in zip(slots, (self.core, 1 - self.core)):
            ref = self.buf.at[self._rows(owner, core)]
            pltpu.make_async_remote_copy(
                ref, ref, self.ssem.at[slot], self.rsem.at[slot], self.group.pair, MESH).wait_recv()
        self._mate(owner)

    def send_mine_up(self):
        self._send_rows(0, self.group.above, self.core)

    def send_mine_down(self):
        self._send_rows(1, self.group.below, self.core)

    def send_mates_up(self):
        self._send_rows(16, self.group.above, 1 - self.core)

    def send_mates_down(self):
        self._send_rows(17, self.group.below, 1 - self.core)

    def take_up2(self):
        self._take_rows((0, 16), BELOW)

    def take_down2(self):
        self._take_rows((1, 17), ABOVE)

    def start(self):
        self.send_own_pair()
        self.send_own_up()
        self.send_own_down()
        self.give_mate()

    def take(self, step):
        if step == 0:
            self._wait(2, PAIR)
            self.send_other_up()
            self.send_other_down()
            self._mate(PAIR)
        elif step == 1:
            self._wait(0, BELOW)
            self.send_far_up()
            self._mate(BELOW)
        elif step == 2:
            self.take_down()
        elif step == 3:
            self.take_other_up()
        elif step == 4:
            self._wait(6, PAIR_ABOVE)
            self.send_far_down()
            self._mate(PAIR_ABOVE)
        elif step == 5:
            self.take_far_up()
        else:
            self.take_far_down()


class Scatter:
    def __init__(self, group, part, terms, rbuf, ssem, rsem):
        self.group, self.part, self.terms, self.ssem, self.rsem = group, part, terms, ssem, rsem
        self.rbuf = rbuf.at[:, pl.ds(*part)]
        self.sent = []

    def at(self, dg, other):
        return span(self.group, (dg, other), self.part)

    def _copy(self, slot, at, device):
        return pltpu.make_async_remote_copy(
            self.terms.at[at], self.rbuf.at[slot], self.ssem.at[slot], self.rsem.at[slot], device, MESH)

    def _send(self, slot, dg, other, device):
        c = self._copy(slot, self.at(dg, other), device)
        c.start()
        self.sent.append(c)

    def _wait(self, slot):
        self._copy(slot, self.at(0, False), self.group.pair).wait_recv()

    def direct(self, *dgs):
        for place in OTHERS + (OWN,):
            if place[0] in dgs and place != OWN:
                self._send(OTHERS.index(seen_from(place)), *place, self.group.device(*place))

    def result_direct(self):
        for slot in range(7):
            self._wait(slot)
        return self.terms[self.at(*OWN)].astype(F32) + sum(self.rbuf[slot].astype(F32) for slot in range(7))

    def far(self):
        self._send(0, 2, False, self.group.above)
        self._send(1, 2, True, self.group.below)

    def near(self):
        self._send(2, 1, True, self.group.above)
        self._send(3, 3, False, self.group.below)

    def fold(self, way):
        dg, other, device = ((1, False, self.group.above), (3, True, self.group.below))[way]
        self._wait(way)
        at = self.at(dg, other)
        self.terms[at] = (self.terms[at].astype(F32) + self.rbuf[way].astype(F32)).astype(BF)
        self._send(way + 4, dg, other, device)

    def _total(self, other):
        direct, folded = (2, 5) if other else (3, 4)
        return (self.terms[self.at(0, other)].astype(F32) + self.rbuf[direct].astype(F32)
                + self.rbuf[folded].astype(F32))

    def cross(self):
        self._wait(2)
        self._wait(5)
        self.terms[self.at(0, True)] = self._total(True).astype(BF)
        self._send(6, 0, True, self.group.pair)

    def result(self):
        self._wait(3)
        self._wait(4)
        own = self._total(False)
        self._wait(6)
        return own + self.rbuf[6].astype(F32)

    def drain(self):
        for c in self.sent:
            c.wait_send()


def kernel(in_ref, pre_ref, w1_ref, w2_ref, og_ref, dxv, out1, out2,
           og_all, in_all, act_all, pre_all, pre_loc, slope, w1, w2, terms, inp, rbuf, rbufx, w1t, w2t,
           og_ss, og_rs, xs_ss, xs_rs, act_ss, act_rs, pre_ss, pre_rs, hid_ss, hid_rs, dx_ss, dx_rs, k_ss, k_rs, l_sem):
    r, c = lax.axis_index("row"), lax.axis_index("col")
    x, zl = r % 4, r // 4
    y, zh, k = c // 4, (c // 2) % 2, c % 2
    mate = (r, c + 1 - 2 * k)
    by_row = Group(x, zl, lambda g, h: (h * 4 + g, c), lambda g, h: h * 4 + g)
    by_col = Group(y, zh, lambda g, h: (r, g * 4 + h * 2 + k), lambda g, h: g * 2 + h)
    mine_row = span(by_row, OWN, (0, T))
    mine_col = span(by_col, OWN, (0, T))
    own64 = pl.ds(pl.multiple_of(k * (T // 2), T // 2), T // 2)

    def units(core):
        return pl.ds(pl.multiple_of(core * U, U), U)

    loads = [
        pltpu.make_async_copy(pre_ref.at[:, units(k)], pre_loc.at[own64], l_sem.at[0]),
        pltpu.make_async_copy(og_ref, og_all.at[k, mine_row], l_sem.at[1]),
        pltpu.make_async_copy(w2_ref.at[units(k)], w2.at[k], l_sem.at[2]),
        pltpu.make_async_copy(in_ref, in_all.at[mine_row], l_sem.at[3]),
        pltpu.make_async_copy(w1_ref, w1, l_sem.at[4]),
    ]
    for load in loads[:3]:
        load.start()

    barrier = pltpu.get_barrier_semaphore()
    friends = (mate, by_col.above, by_col.below, by_col.pair) + tuple(by_row.device(*place) for place in OTHERS)
    for friend in friends:
        pl.semaphore_signal(barrier, inc=1, device_id=friend, device_id_type=MESH)
    og = [Gather(by_row, part, og_all.at[k], og_all.at[1 - k], mate, og_ss.at[i], og_rs.at[i], og_ref.at[pl.ds(*part)])
          for i, part in enumerate(PARTS)]
    xs = [Gather(by_row, part, in_all, None, None, xs_ss.at[i], xs_rs.at[i], in_ref.at[pl.ds(*part)])
          for i, part in enumerate(XPARTS)]
    act = [Gather(by_col, (0, T), act_all.at[k, f], act_all.at[1 - k, f], mate, act_ss.at[f], act_rs.at[f],
                  core=k)
           for f in range(F)]
    pre = [Gather(by_col, part, pre_all.at[k], pre_all.at[1 - k], mate, pre_ss.at[i], pre_rs.at[i])
           for i, part in enumerate(PARTS)]
    hid = [Scatter(by_col, part, terms, rbuf, hid_ss.at[i], hid_rs.at[i]) for i, part in enumerate(PARTS)]
    dx = [Scatter(by_row, part, inp, rbufx, dx_ss.at[i], dx_rs.at[i]) for i, part in enumerate(PARTS)]

    to_mate = [
        pltpu.make_async_remote_copy(
            pre_ref.at[:, units(1 - k)], pre_loc.at[own64], k_ss.at[0], k_rs.at[0], mate, MESH),
        pltpu.make_async_remote_copy(w2_ref.at[units(1 - k)], w2.at[k], k_ss.at[1], k_rs.at[1], mate, MESH),
    ]

    def activate(f, core):
        tokens = pl.ds(pl.multiple_of(core * (T // 2), T // 2), T // 2)
        own = act[f]._rows(OWN, core)

        def some(n, _):
            at = pl.ds(pl.multiple_of(f * V + n * 128, 128), 128)
            to = pl.ds(pl.multiple_of(n * 128, 128), 128)
            a = pre_loc[tokens, at].astype(F32)
            t = jnp.tanh(ROOT * (a + CUBE * (a * a * a)))
            act_all[k, f, own, to] = (0.5 * a * (1.0 + t)).astype(BF)
            slope[tokens, at] = 0.5 * (1.0 + t) + 0.5 * a * (1.0 - t * t) * (ROOT * (1.0 + 3.0 * CUBE * (a * a)))
            return 0

        lax.fori_loop(0, V // 128, some, 0)

    def pre_grad(s):
        grad = hid[s].result().astype(BF).astype(F32)
        pre_all[k, span(by_col, OWN, PARTS[s])] = (slope[pl.ds(*PARTS[s])] * grad).astype(BF)

    def blocks(scatter, dgs):
        return [scatter.at(dg, other) for dg in dgs for other in (False, True)]

    def product(scatter, dgs, lefts, rights, width, out):
        places, size = blocks(scatter, dgs), scatter.part[1]
        lefts = [jnp.concatenate([left[at] for at in places], axis=0) for left in lefts]
        for n in range(width // 256):
            to = pl.ds(n * 256, 256)
            total = sum(dot(left, right[:, to]) for left, right in zip(lefts, rights)).astype(BF)
            for i, at in enumerate(places):
                out[at, to] = total[i * size:(i + 1) * size]

    def hidden(s, *dgs):
        product(hid[s], dgs, [og_all.at[core] for core in (0, 1)], [w2t.at[core] for core in (0, 1)], U, terms)

    def input_part(s, *dgs):
        product(dx[s], dgs, [pre_all.at[core] for core in (0, 1)], [w1t.at[pl.ds(core * U, U)] for core in (0, 1)], W, inp)

    def second_grad(core, f):
        out2[pl.ds(core * U + f * V, V)] = tl_dot(act_all[core, f], og_all[k]).astype(BF)

    def first_grad(n):
        out1[:, pl.ds(n * W, W)] = tl_dot(in_all[...], pre_all[n // 2, :, pl.ds((n % 2) * W, W)]).astype(BF)

    def input_grad(s, direct=False):
        dxv[pl.ds(*PARTS[s])] = (dx[s].result_direct() if direct else dx[s].result()).astype(BF)

    loads[0].wait()
    for f in range(F):
        activate(f, k)
    pl.semaphore_wait(barrier, len(friends))

    to_mate[0].start()
    act[3].send_mine_down()
    og[0].start_direct()
    act[0].send_mine_up()
    act[1].send_mine_down()
    to_mate[0].wait_recv()
    activate(0, 1 - k)
    to_mate[1].start()
    act[0].send_mates_up()
    activate(1, 1 - k)
    act[2].send_mine_down()
    act[1].send_mates_down()
    activate(2, 1 - k)
    act[2].send_mates_up()
    for load in loads[3:]:
        load.start()
    activate(3, 1 - k)
    act[0].send_mine_down()
    og[1].start()
    act[1].send_mine_up()
    loads[2].wait()
    w2t[k] = w2[k].T
    og[0].take_direct(0)
    act[3].send_mates_down()
    act[0].send_mates_down()
    act[1].send_mates_up()
    act[0].send_own_pair()
    act[0].take_up2()
    act[3].send_mates_up()
    act[2].send_mates_down()
    act[1].take_down2()
    og[0].take_direct(6)
    xs[0].send_own_pair()
    xs[1].send_own_pair()
    og[0].take_direct(5)
    act[3].send_mine_up()
    to_mate[1].wait_recv()
    w2t[1 - k] = w2[1 - k].T
    og[0].take_direct(2)
    act[0].send_half_up()
    xs[1].send_own_up()
    act[1].send_half_down()
    og[0].take_direct(1)
    act[1].take_up2()
    act[2].send_mine_up()
    act[3].take_down2()
    act[1].send_half_up()
    og[0].take_direct(3)
    og[0].take_direct(4)
    act[0].take_down2()
    act[1].send_own_pair()
    act[3].send_half_down()
    act[0].send_half_down()
    og[1].take(0)
    og[0].take_mate()
    loads[1].wait()
    hidden(0, 2)
    hid[0].far()
    hidden(0, 1, 3, 0)
    hid[0].near()
    og[1].take(4)
    og[1].take(1)
    og[1].take(3)
    og[2].start()
    act[0].send_pair_up()
    hid[0].fold(1)
    act[0].send_pair_down()
    xs[1].take_up()
    hid[0].fold(0)
    og[1].take(6)
    act[1].send_pair_up()
    og[1].take(5)
    xs[0].take_pair()
    og[1].take(2)
    xs[1].take_pair()
    act[0].take_far()
    og[2].take(1)
    og[2].take(0)
    og[1].take_mate()
    hidden(1, 2)
    hid[1].far()
    loads[4].wait()
    w1t[...] = w1[...].T
    act[3].take_up2()
    hidden(1, 1, 3, 0)
    hid[1].near()
    hid[0].cross()
    xs[1].send_other_down()
    og[2].take(4)
    og[2].take(3)
    act[3].send_pair_down()
    act[0].send_pair_far()
    og[2].take(5)
    act[3].send_half_up()
    xs[0].send_other_down()
    hid[1].fold(1)
    hid[1].fold(0)
    og[2].take(6)
    act[1].give_mate()
    pre_grad(0)
    pre[0].start()
    og[2].take(2)
    og[2].take_mate()
    act[0].give_mate()
    hidden(2, 2)
    hid[2].far()
    hid[1].cross()
    hidden(2, 1, 3, 0)
    hid[2].near()
    act[0].take_pair_up()
    act[3].give_mate()
    act[1].take_pair_up()
    act[1].send_pair_down()
    pre[0].take(0)
    xs[1].send_far_up()
    act[1].take_pair()
    loads[3].wait()
    xs[0].send_own_up()
    act[1].take_far()
    hid[2].fold(1)
    xs[1].send_own_down()
    act[0].take_pair_down()
    act[2].take_down2()
    act[2].take_up2()
    act[0].take_pair()
    act[3].send_own_pair()
    act[3].send_pair_up()
    act[3].take_far()
    pre[0].take(2)
    pre[0].take(1)
    xs[0].send_other_up()
    hid[2].fold(0)
    act[0].take_pair_far()
    pre[0].take(4)
    act[0].take_mate()
    pre_grad(1)
    pre[1].start()
    act[2].give_mate()
    second_grad(0, 0)
    second_grad(1, 0)
    xs[0].take_other_up()
    hid[2].cross()
    xs[0].take_up()
    pre[0].take(3)
    xs[1].send_other_up()
    act[1].send_pair_far()
    xs[1].take_other_down()
    xs[1].send_far_down()
    pre[0].take(5)
    pre[0].take(6)
    act[3].take_pair_down()
    xs[0].take_other_down()
    act[1].take_pair_down()
    act[3].send_pair_far()
    pre[1].take(0)
    xs[1].take_other_up()
    xs[0].send_far_down()
    xs[0].send_far_up()
    pre[0].take_mate()
    input_part(0, 2)
    dx[0].far()
    pre_grad(2)
    pre[2].start()
    pre[1].take(2)
    input_part(0, 1, 3, 0)
    dx[0].near()
    act[1].take_pair_far()
    pre[1].take(1)
    pre[1].take(4)
    xs[1].take_far_up()
    xs[1].take_far_down()
    xs[0].send_own_down()
    act[3].take_pair_up()
    act[2].send_own_pair()
    xs[0].take_far_down()
    act[3].take_pair()
    act[1].take_mate()
    second_grad(1, 1)
    act[3].take_pair_far()
    dx[0].fold(1)
    pre[1].take(3)
    act[2].send_pair_up()
    pre[2].take(0)
    pre[2].take(1)
    act[2].send_half_up()
    pre[2].take(2)
    second_grad(0, 1)
    dx[0].fold(0)
    act[3].take_mate()
    xs[0].take_far_up()
    pre[1].take(6)
    act[2].send_pair_down()
    act[2].send_half_down()
    pre[1].take(5)
    xs[0].take_down()
    second_grad(1, 3)
    act[2].take_pair()
    pre[2].take(4)
    dx[0].cross()
    xs[1].take_down()
    act[2].take_pair_up()
    pre[1].take_mate()
    input_part(1, 2)
    dx[1].far()
    pre[2].take(3)
    act[2].take_pair_down()
    input_part(1, 1, 3, 0)
    dx[1].near()
    pre[2].take(5)
    input_grad(0)
    pre[2].take(6)
    second_grad(0, 3)
    act[2].take_far()
    act[2].send_pair_far()
    dx[1].fold(0)
    dx[1].fold(1)
    pre[2].take_mate()
    input_part(2, 2)
    dx[2].direct(2)
    input_part(2, 1, 3, 0)
    dx[2].direct(1, 3, 0)
    first_grad(3)
    dx[1].cross()
    act[2].take_pair_far()
    first_grad(0)
    first_grad(2)
    act[2].take_mate()
    second_grad(0, 2)
    second_grad(1, 2)
    first_grad(1)
    input_grad(1)
    for item in (*og, *xs, *act, *pre, *hid, *dx[:-1]):
        item.drain()
    for copy in to_mate:
        copy.wait_send()
    input_grad(2, True)
    dx[-1].drain()


def write_out(dx, dw1, dw2, dx_out, dw1_out, dw2_out, sems):
    copies = []
    for src, dst in ((dw1, dw1_out), (dw2, dw2_out), (dx, dx_out)):
        rows = src.shape[0] // 4
        for at in (pl.ds(n * rows, rows) for n in range(4)):
            copies.append(pltpu.make_async_copy(src.at[at], dst.at[at], sems.at[len(copies)]))
    for copy in copies:
        copy.start()
    for copy in copies:
        copy.wait()


def local(inputs, pre_act, w_first, w_second, out_grad):
    sem, S, X = pltpu.SemaphoreType.DMA, len(PARTS), len(XPARTS)
    vm = lambda *shape, dtype=BF: pltpu.VMEM(shape, dtype)
    results = pl.pallas_call(
        kernel,
        out_shape=(
            pltpu.VMEM((T, W), BF),
            pltpu.VMEM((W, 2 * U), BF),
            pltpu.VMEM((2 * U, W), BF),
        ),
        in_specs=[pl.BlockSpec(memory_space=pl.ANY)] * 5,
        out_specs=[pl.BlockSpec(memory_space=pltpu.VMEM)] * 3,
        scratch_shapes=[
            vm(2, N, W),
            vm(N, W),
            vm(2, F, N, V),
            vm(2, N, U),
            vm(T, U),
            vm(T, U, dtype=F32),
            vm(W, 2 * U),
            vm(2, U, W),
            vm(N, U),
            vm(N, W),
            vm(7, T, U),
            vm(7, T, W),
            vm(2 * U, W),
            vm(2, W, U),
            sem((S, 16)), sem((S, 16)), sem((X, 7)), sem((X, 7)), sem((F, 18)), sem((F, 18)), sem((S, 16)), sem((S, 16)),
            sem((S, 7)), sem((S, 7)), sem((S, 7)), sem((S, 7)), sem((2,)), sem((2,)), sem((5,)),
        ],
        compiler_params=pltpu.CompilerParams(
            collective_id=0, has_side_effects=True, vmem_limit_bytes=50 * 2**20
        ),
        cost_estimate=pl.CostEstimate(flops=19_327_352_832, bytes_accessed=20_000_000, transcendentals=400_000),
        name="ffn_back",
    )(inputs, pre_act, w_first, w_second, out_grad)
    return pl.pallas_call(
        write_out,
        out_shape=[jax.ShapeDtypeStruct(array.shape, BF) for array in results],
        in_specs=[pl.BlockSpec(memory_space=pltpu.VMEM)] * 3,
        out_specs=[pl.BlockSpec(memory_space=pl.ANY)] * 3,
        scratch_shapes=[sem((12,))],
        compiler_params=pltpu.CompilerParams(vmem_limit_bytes=1024 * 1024),
        name="write_out",
    )(*results)


def solution(mesh):
    placed = (P("row", "col"), P("col", "row"), P("col", "row"), P("row", "col"), P("row", "col"))
    return jax.shard_map(
        local,
        mesh=mesh,
        in_specs=placed,
        out_specs=(P("row", "col"), P("col", "row"), P("row", "col")),
        check_vma=False,
    )
```
